256 devices in a mesh: gx: 32 (over y, x, core), gy: 8 (over z).
Axes of the slice: x: 4, y: 4, z: 8, core: 2. Of those that a mesh axis runs over, the one named last changes fastest.
Arguments:
- embeddings: bfloat16 [262144, 1024], P(('gx', 'gy')), may hold values from -60 to 60
- cluster: int32 [262144], replicated, may hold values from 0 to 511, never falling along the last dimension, each value on 1 to 4096 neighbouring positions
Outputs:
- log_cover: float32 [262144], P(('gx', 'gy'))
- relative_cover: float32 [262144], P(('gx', 'gy'))
The draws below stay inside these ranges and needn't reach their ends.
Inputs may be any that keep to these rules, and one draw needn't show every extreme that they name: cluster numbers never fall along the rows; each cluster holds 1 to 4096 rows and one holds exactly that many.
All inputs are finite; a program needn't handle non-finite values.
Results may differ from the reference program's by a relative error of at most 0.002.
Values may be sent and summed in bfloat16 or wider, within the bound.
A program may use at most 64 MiB of HBM per device.

```python
import math
import jax
import jax.numpy as jnp
import numpy as np
from jax import lax

D = 1024
ROWS_DEV = 1024
REACH = 4
ROWS = 262144
CLUSTERS = 512
DEVICES = 256


def draw_embeddings(key, part):
    key_base = jax.random.fold_in(key, 11)
    key_common = jax.random.fold_in(key, 14)
    key_lift = jax.random.fold_in(key, 15)
    normal_base = jnp.clip(jax.random.normal(key_base, (ROWS, D), jnp.float32), -6.0, 6.0)
    common = jnp.clip(jax.random.normal(key_common, (D,), jnp.float32), -6.0, 6.0)
    row_ids = jnp.arange(ROWS)
    block_ids = row_ids // ROWS_DEV
    block_lift = jax.random.uniform(key_lift, (ROWS // ROWS_DEV,), jnp.float32, 0.0, 0.6)
    result = jnp.clip(normal_base + block_lift[block_ids][:, None] * common[None, :], -6.0, 6.0)
    return result.astype(jnp.bfloat16)


def profile(amount, total, most, lean):
    weights = [(1 << 20) // math.isqrt(standing ** lean) + 1 for standing in range(2, amount + 1)]
    surplus, holding = total - most - (amount - 1), [1] * (amount - 1)
    while surplus > 0:
        movable = [i for i in range(amount - 1) if holding[i] < most]
        pool, left = sum([weights[i] for i in movable]), surplus
        for i in movable:
            more = min(most - holding[i], max(1, left * weights[i] // pool), surplus)
            holding[i] = holding[i] + more
            surplus = surplus - more
    return np.array([most] + holding)


def ragged(key, amount, total, bound, lean):
    if amount == 2:
        one = jax.random.randint(key, (), max(1, total - bound), min(bound, total - 1) + 1)
        return jnp.stack([one, total - one])
    tallies = jnp.asarray(profile(amount, total, bound, lean), jnp.int32)
    twos = (amount - 1) // 2
    donor, receiver = tallies[1:1 + 2 * twos:2], tallies[2:2 + 2 * twos:2]
    margin = jnp.minimum(donor - 1, bound - receiver)
    passed = jax.random.randint(jax.random.fold_in(key, 1), (twos,), 0, 1 << 20) % (margin + 1)
    tallies = tallies.at[1:1 + 2 * twos:2].set(donor - passed).at[2:2 + 2 * twos:2].set(receiver + passed)
    return tallies[jax.random.permutation(jax.random.fold_in(key, 2), amount)]


def setup_inputs(seed: int = 0) -> dict:
    key_of = jax.random.split(jax.random.key(seed), 3)
    embeddings = draw_embeddings(jax.random.fold_in(key_of[2], 71), 0)
    cluster = jnp.searchsorted(jnp.cumsum(ragged(key_of[1], CLUSTERS, ROWS, REACH * ROWS_DEV, 2)), jnp.arange(ROWS), side="right").astype(jnp.int32)
    return dict(embeddings=embeddings, cluster=cluster)


INVERSE_TEMP = 100.0
FLOOR_SCORE = -1e+30
EPSILON = 1e-06

def unit_rows(embeddings):
    values = embeddings.astype(jnp.float32)
    scale = lax.rsqrt(lax.optimization_barrier(jnp.sum(values * values, axis=1, keepdims=True)) + EPSILON)
    return (values * scale).astype(jnp.bfloat16)

def combine(first, second):
    top = jnp.maximum(first[0], second[0])
    total = first[1] * jnp.exp(first[0] - top) + second[1] * jnp.exp(second[0] - top)
    return (top, total)

def tile_parts(left_block, right_block, left_tags, right_tags, diagonal):
    scores = lax.dot_general(left_block, right_block, (((1,), (1,)), ((), ())), preferred_element_type=jnp.float32) * INVERSE_TEMP
    is_live = left_tags[:, None] == right_tags[None, :]
    if diagonal:
        size_rows = left_block.shape[0]
        is_live = is_live & (jnp.arange(size_rows)[:, None] != jnp.arange(size_rows)[None, :])
    masked = jnp.where(is_live, scores, FLOOR_SCORE)
    row_max = lax.optimization_barrier(jnp.max(masked, axis=1))
    col_max = lax.optimization_barrier(jnp.max(masked, axis=0))
    row_sum = lax.optimization_barrier(jnp.sum(jnp.where(is_live, jnp.exp(masked - row_max[:, None]), 0.0), axis=1))
    col_sum = lax.optimization_barrier(jnp.sum(jnp.where(is_live, jnp.exp(masked - col_max[None, :]), 0.0), axis=0))
    return ((row_max, row_sum), (col_max, col_sum))

def finish(part):
    top = jnp.maximum(part[0], 0.0)
    return top + jnp.log(jnp.exp(-top) + part[1] * jnp.exp(part[0] - top))

def reference(embeddings, cluster):
    unit_block = unit_rows(embeddings)
    cluster_tags = cluster + 1
    pad_unit = jnp.concatenate([unit_block, jnp.zeros((REACH * ROWS_DEV, D), jnp.bfloat16)], axis=0)
    pad_tags = jnp.concatenate([cluster_tags, jnp.zeros((REACH * ROWS_DEV,), jnp.int32)], axis=0)

    def one_block(block_index):
        first_row = (block_index * ROWS_DEV).astype(jnp.int32)
        left_block = lax.dynamic_slice_in_dim(pad_unit, first_row, ROWS_DEV, 0)
        left_tags = lax.dynamic_slice_in_dim(pad_tags, first_row, ROWS_DEV, 0)
        row_part, unused = tile_parts(left_block, left_block, left_tags, left_tags, True)
        col_tops = []
        col_totals = []
        for offset in range(1, REACH + 1):
            right_row = (first_row + offset * ROWS_DEV).astype(jnp.int32)
            right_block = lax.dynamic_slice_in_dim(pad_unit, right_row, ROWS_DEV, 0)
            right_tags = lax.dynamic_slice_in_dim(pad_tags, right_row, ROWS_DEV, 0)
            side_row, side_col = tile_parts(left_block, right_block, left_tags, right_tags, False)
            row_part = combine(row_part, side_row)
            col_tops.append(side_col[0])
            col_totals.append(side_col[1])
        return (row_part[0], row_part[1], jnp.stack(col_tops), jnp.stack(col_totals))
    row_tops, row_totals, col_tops, col_totals = lax.map(one_block, jnp.arange(DEVICES, dtype=jnp.int32))
    part = (row_tops, row_totals)
    for offset in range(1, REACH + 1):
        empty = jnp.zeros((offset, ROWS_DEV), jnp.float32)
        moved_tops = jnp.concatenate([empty, col_tops[:DEVICES - offset, offset - 1]], axis=0)
        moved_totals = jnp.concatenate([empty, col_totals[:DEVICES - offset, offset - 1]], axis=0)
        part = combine(part, (moved_tops, moved_totals))
    log_cover = finish(part).reshape(ROWS)
    cluster_sums = jax.ops.segment_sum(log_cover, cluster, num_segments=CLUSTERS)
    cluster_counts = jax.ops.segment_sum(jnp.ones((ROWS,), jnp.float32), cluster, num_segments=CLUSTERS)
    cluster_mean = cluster_sums / cluster_counts
    relative_cover = log_cover - cluster_mean[cluster]
    return (log_cover, relative_cover)
```

```python
import math

import jax
import jax.numpy as jnp
from jax import lax
from jax.experimental import pallas as pl
from jax.experimental.pallas import tpu as pltpu
from jax.sharding import PartitionSpec as P

MESH = pl.DeviceIdType.MESH
INVERSE_TEMP = 100.0
EPSILON = 1e-06
SHIFT = 32.0
GAIN = INVERSE_TEMP * math.log2(math.e)
DROP = SHIFT * math.log2(math.e)

ROWS = 1024
CHUNK = 128
CHUNKS = ROWS // CHUNK
LEFT, RIGHT = 0, 1
REACH = 4


def chunk_rows(c):
    return pl.ds(pl.multiple_of(c * CHUNK, CHUNK), CHUNK)


def across(row):
    return jnp.transpose(jnp.broadcast_to(row, (CHUNK, CHUNK)))


def scores_of(left, right):
    return lax.dot_general(left, right, (((1,), (1,)), ((), ())), preferred_element_type=jnp.float32)


def kernel(
    x_ref, cluster_ref, cover_ref, relative_ref,
    raw, own, near, far, tags, columns, row_sums, col_sums, parts, parts_in, sums, sums_in,
    raw_sem, tags_sem, own_send, relay_send, near_recv, far_recv, parts_send, parts_recv, sums_send, sums_recv,
):
    sizes = (lax.axis_size("gx"), lax.axis_size("gy"))
    devices = sizes[0] * sizes[1]
    me = lax.axis_index("gx") * sizes[1] + lax.axis_index("gy")

    def block(offset):
        return lax.rem(me + (offset + devices), devices)

    def device(offset):
        place = block(offset)
        return (place // sizes[1], lax.rem(place, sizes[1]))

    def raw_copy(c):
        return pltpu.make_async_copy(x_ref.at[chunk_rows(c)], raw.at[chunk_rows(c)], raw_sem.at[c])

    def tags_copy(k):
        return pltpu.make_async_copy(cluster_ref.at[block(k - REACH)], tags.at[k], tags_sem.at[k])

    def own_copy(side, c):
        return pltpu.make_async_remote_copy(
            src_ref=own.at[chunk_rows(c)], dst_ref=near.at[side, chunk_rows(c)],
            send_sem=own_send.at[side, c], recv_sem=near_recv.at[side, c],
            device_id=device(1 if side == LEFT else -1), device_id_type=MESH,
        )

    def relay_copy(side, c):
        return pltpu.make_async_remote_copy(
            src_ref=near.at[side, chunk_rows(c)], dst_ref=far.at[side, chunk_rows(c)],
            send_sem=relay_send.at[side, c], recv_sem=far_recv.at[side, c],
            device_id=device(1 if side == LEFT else -1), device_id_type=MESH,
        )

    steps = [7, 0, 6, 1, 5, 2, 4, 3]
    for c in steps:
        raw_copy(c).start()
    for k in range(2 * REACH + 1):
        tags_copy(k).start()

    barrier = pltpu.get_barrier_semaphore()
    others = [k for k in range(-REACH, REACH + 1) if k != 0]
    for k in others:
        pl.semaphore_signal(barrier, inc=1, device_id=device(k), device_id_type=MESH)
    row_sums[...] = jnp.zeros_like(row_sums)
    col_sums[...] = jnp.zeros_like(col_sums)

    def normalise(c):
        raw_copy(c).wait()

        def some(g, carry):
            rows = pl.ds(pl.multiple_of(c * CHUNK + g * 16, 16), 16)
            values = raw[rows].astype(jnp.float32)
            scale = lax.rsqrt(jnp.sum(values * values, axis=1, keepdims=True) + EPSILON)
            own[rows] = (values * scale).astype(jnp.bfloat16)
            return carry

        lax.fori_loop(0, CHUNK // 16, some, 0, unroll=2)

    normalise(7)
    normalise(0)
    pl.semaphore_wait(barrier, len(others))
    own_copy(LEFT, 7).start()
    own_copy(RIGHT, 0).start()
    for n in range(1, 4):
        normalise(7 - n)
        normalise(n)
        own_copy(LEFT, 7 - n).start()
        own_copy(RIGHT, n).start()
    for n in range(4, CHUNKS):
        own_copy(LEFT, 7 - n).start()
        own_copy(RIGHT, n).start()

    for k in range(2 * REACH + 1):
        tags_copy(k).wait()

    def columns_of(c, carry):
        for k in range(5):
            columns[k, chunk_rows(c)] = across(tags[k + 2, pl.ds(c, 1), :])
        return carry

    lax.fori_loop(0, CHUNKS, columns_of, 0)

    def piece(down, down_tags, right_ref, tag_row, first, width, row_at, col_at, same=None):
        right = right_ref[pl.ds(pl.multiple_of(first * CHUNK, CHUNK), width * CHUNK)]
        scores = scores_of(down, right)
        total = None
        for w in range(width):
            live = down_tags == tags[tag_row, pl.ds(first + w, 1), :]
            if same is not None:
                distinct = lax.broadcasted_iota(jnp.int32, (CHUNK, CHUNK), 0) + (same - (first + w)) * CHUNK
                live = live & (distinct != lax.broadcasted_iota(jnp.int32, (CHUNK, CHUNK), 1))
            cover = jnp.where(live, jnp.exp2(scores[:, w * CHUNK : (w + 1) * CHUNK] * GAIN - DROP), 0.0)
            if row_at is not None:
                total = cover if total is None else total + cover
            col_sums[col_at, first + w] += jnp.sum(cover.reshape(CHUNK // 8, 8, CHUNK), axis=0)
        if row_at is not None:
            which, c = row_at
            row_sums[which, chunk_rows(c)] += total

    def strip(down_ref, down_at, c, right_ref, right_at, row_which, col_at, diagonal=False):
        down = down_ref[chunk_rows(c)]
        down_tags = columns[down_at + 2, chunk_rows(c)]
        for first in range(0, CHUNKS, 2):
            piece(
                down, down_tags, right_ref, right_at + REACH, first, 2,
                None if row_which is None else (row_which, c), col_at, c if diagonal else None,
            )

    left1, left2, right1, right2 = near.at[LEFT], far.at[LEFT], near.at[RIGHT], far.at[RIGHT]
    ROW_L1, ROW_R1, ROW_R2 = 0, 1, 2
    COL_S, COL_L1, COL_L2 = 0, 1, 2

    def diagonal_step(c, carry):
        strip(own, 0, c, own, 0, None, COL_S, diagonal=True)
        return carry

    lax.fori_loop(0, CHUNKS, diagonal_step, 0)

    def near_step(n, carry):
        own_copy(LEFT, 7 - n).wait_recv()
        relay_copy(LEFT, 7 - n).start()
        own_copy(RIGHT, n).wait_recv()
        relay_copy(RIGHT, n).start()
        strip(left1, -1, 7 - n, own, 0, ROW_L1, COL_S)
        return carry

    lax.fori_loop(0, CHUNKS, near_step, 0)

    def middle_step(c, carry):
        strip(right1, 1, c, left1, -1, ROW_R1, COL_L1)
        return carry

    lax.fori_loop(0, CHUNKS, middle_step, 0)

    def corner(c, d):
        piece(right2[chunk_rows(c)], columns[4, chunk_rows(c)], left2, REACH - 2, d, 1, (ROW_R2, c), COL_L2)

    def far_step(n, carry):
        relay_copy(RIGHT, n).wait_recv()
        strip(right2, 2, n, left1, -1, ROW_R2, COL_L1)
        relay_copy(LEFT, 7 - n).wait_recv()

        def new_right(d, inner):
            corner(n, d)
            return inner

        def new_left(c, inner):
            corner(c, 7 - n)
            return inner

        lax.fori_loop(jnp.maximum(n, 7 - n), CHUNKS, new_right, 0)
        lax.fori_loop(0, jnp.minimum(n, 8 - n), new_left, 0)
        return carry

    lax.fori_loop(0, CHUNKS, far_step, 0)

    for c in range(CHUNKS):
        rows = slice(c * CHUNK, (c + 1) * CHUNK)
        lane = slice(c, c + 1)
        down = [jnp.sum(jnp.transpose(row_sums[k, rows]), axis=0, keepdims=True) for k in range(3)]
        side = [jnp.sum(col_sums[k, c], axis=0, keepdims=True) for k in range(3)]
        parts[0, lane] = side[COL_L2]
        parts[1, lane] = down[ROW_L1] + side[COL_L1]
        parts[2, lane] = down[ROW_R1]
        parts[3, lane] = down[ROW_R2]
        parts[4, lane] = side[COL_S]

    part_offsets = [-2, -1, 1, 2]

    def parts_copy(k):
        return pltpu.make_async_remote_copy(
            src_ref=parts.at[k], dst_ref=parts_in.at[k], send_sem=parts_send.at[k], recv_sem=parts_recv.at[k],
            device_id=device(part_offsets[k]), device_id_type=MESH,
        )

    for k in range(4):
        parts_copy(k).start()

    mine = tags[REACH]
    zero = jnp.zeros((CHUNKS, CHUNK), jnp.float32)

    def edge_tag(k):
        at = tags[k + REACH, CHUNKS - 1 : CHUNKS, CHUNK - 1 : CHUNK] if k < 0 else tags[k + REACH, 0:1, 0:1]
        return jnp.broadcast_to(at, (CHUNKS, CHUNK))

    def total_of(values):
        return jnp.broadcast_to(jnp.sum(values, keepdims=True), (CHUNKS, CHUNK))

    def own_totals(column_values):
        totals = []
        for j in range(CHUNKS):

            def add(c, acc):
                same = columns[2, chunk_rows(c)] == tags[REACH, j : j + 1, :]
                picked = jnp.where(same, column_values(c), 0.0)
                return acc + jnp.sum(picked.reshape(CHUNK // 8, 8, CHUNK), axis=0)

            acc = lax.fori_loop(0, CHUNKS, add, jnp.zeros((8, CHUNK), jnp.float32), unroll=True)
            totals.append(jnp.sum(acc, axis=0, keepdims=True))
        return jnp.concatenate(totals, axis=0)

    counts = own_totals(lambda c: 1.0)
    for k in others:
        edge = edge_tag(k)
        many = total_of(jnp.where(tags[k + REACH] == edge, 1.0, 0.0))
        counts = counts + jnp.where(mine == edge, many, 0.0)

    total = parts[4]
    for k in range(4):
        parts_copy(k).wait_recv()
        total = total + parts_in[k]
    cover = jnp.where(
        total < math.exp(-SHIFT),
        jnp.log1p(jnp.minimum(total, math.exp(-SHIFT)) * math.exp(SHIFT)),
        SHIFT + jnp.log(total + math.exp(-SHIFT)),
    )
    cover_ref[...] = cover

    first_tag = jnp.broadcast_to(mine[0:1, 0:1], (CHUNKS, CHUNK))
    last_tag = jnp.broadcast_to(mine[CHUNKS - 1 : CHUNKS, CHUNK - 1 : CHUNK], (CHUNKS, CHUNK))
    sums[0] = total_of(jnp.where(mine == first_tag, cover, zero))
    sums[1] = total_of(jnp.where(mine == last_tag, cover, zero))

    def sums_copy(k):
        at = others.index(k)
        return pltpu.make_async_remote_copy(
            src_ref=sums.at[0 if k < 0 else 1], dst_ref=sums_in.at[at], send_sem=sums_send.at[at], recv_sem=sums_recv.at[at],
            device_id=device(k), device_id_type=MESH,
        )

    for k in others:
        sums_copy(k).start()
    for c in range(CHUNKS):
        row_sums[0, c * CHUNK : (c + 1) * CHUNK] = across(cover[c : c + 1])
    cluster_sums = own_totals(lambda c: row_sums[0, chunk_rows(c)])
    for k in others:
        sums_copy(k).wait_recv()
        cluster_sums = cluster_sums + jnp.where(mine == edge_tag(-k), sums_in[others.index(k)], zero)
    relative_ref[...] = cover - cluster_sums / counts

    for side in (LEFT, RIGHT):
        for c in range(CHUNKS):
            own_copy(side, c).wait_send()
            relay_copy(side, c).wait_send()
    for k in range(4):
        parts_copy(k).wait_send()
    for k in others:
        sums_copy(k).wait_send()


def per_device(embeddings, cluster):
    rows, width = embeddings.shape
    vmem = pl.BlockSpec(memory_space=pltpu.VMEM)
    anywhere = pl.BlockSpec(memory_space=pltpu.HBM)
    dma = pltpu.SemaphoreType.DMA
    cover, relative = pl.pallas_call(
        kernel,
        out_shape=[jax.ShapeDtypeStruct((CHUNKS, CHUNK), jnp.float32)] * 2,
        in_specs=[anywhere, anywhere],
        out_specs=[vmem, vmem],
        scratch_shapes=[
            pltpu.VMEM((rows, width), jnp.bfloat16),
            pltpu.VMEM((rows, width), jnp.bfloat16),
            pltpu.VMEM((2, rows, width), jnp.bfloat16),
            pltpu.VMEM((2, rows, width), jnp.bfloat16),
            pltpu.VMEM((2 * REACH + 1, CHUNKS, CHUNK), jnp.int32),
            pltpu.VMEM((5, rows, CHUNK), jnp.int32),
            pltpu.VMEM((3, rows, CHUNK), jnp.float32),
            pltpu.VMEM((3, CHUNKS, 8, CHUNK), jnp.float32),
            pltpu.VMEM((5, CHUNKS, CHUNK), jnp.float32),
            pltpu.VMEM((4, CHUNKS, CHUNK), jnp.float32),
            pltpu.VMEM((2, CHUNKS, CHUNK), jnp.float32),
            pltpu.VMEM((2 * REACH, CHUNKS, CHUNK), jnp.float32),
            dma((CHUNKS,)),
            dma((2 * REACH + 1,)),
            dma((2, CHUNKS)),
            dma((2, CHUNKS)),
            dma((2, CHUNKS)),
            dma((2, CHUNKS)),
            dma((4,)),
            dma((4,)),
            dma((2 * REACH,)),
            dma((2 * REACH,)),
        ],
        compiler_params=pltpu.CompilerParams(
            collective_id=0, has_side_effects=True, vmem_limit_bytes=40 << 20
        ),
        name="cover",
    )(embeddings, cluster.reshape(-1, CHUNKS, CHUNK))
    return cover.reshape(rows), relative.reshape(rows)


def solution(mesh):
    placed = (P(("gx", "gy"), None), P())
    return jax.shard_map(
        per_device,
        mesh=mesh,
        in_specs=placed,
        out_specs=(P(("gx", "gy")), P(("gx", "gy"))),
        check_vma=False,
    )
```

```python
import math

import jax
import jax.numpy as jnp
from jax import lax
from jax.experimental import pallas as pl
from jax.experimental.pallas import tpu as pltpu
from jax.sharding import PartitionSpec as P

MESH = pl.DeviceIdType.MESH
INVERSE_TEMP = 100.0
EPSILON = 1e-06
SHIFT = 32.0
GAIN = INVERSE_TEMP * math.log2(math.e)
DROP = SHIFT * math.log2(math.e)

ROWS = 1024
CHUNK = 128
CHUNKS = ROWS // CHUNK
LEFT, RIGHT = 0, 1
REACH = 4
PERIOD = 16

S, C1, C2, C3, P1, P2, X = REACH, REACH + 1, REACH + 2, REACH + 3, REACH - 1, REACH - 2, 2 * REACH + 1
AWAY = 6
PART_OFFSETS = [-AWAY, -3, -2, -1, 1, 2, 3, AWAY]
COLUMNS = {S: 0, C1: 1, C2: 2, C3: 3, P1: 4, P2: 5}
DOWN = {C1: 0, C2: 1, C3: 2, P1: 3, P2: 4}
ACROSS = {S: 0, C1: 1, C2: 2, P1: 3, X: 4}


def chunk_rows(c):
    return pl.ds(pl.multiple_of(c * CHUNK, CHUNK), CHUNK)


def across(row):
    return jnp.transpose(jnp.broadcast_to(row, (CHUNK, CHUNK)))


def scores_of(left, right):
    return lax.dot_general(left, right, (((1,), (1,)), ((), ())), preferred_element_type=jnp.float32)


def each_chunk(body):
    def step(c, carry):
        body(c)
        return carry

    lax.fori_loop(0, CHUNKS, step, 0)


def kernel(
    x_ref, cluster_ref, cover_ref, relative_ref,
    raw, own, near, far, third, other, tags, columns, row_sums, col_sums, own_part, parts, parts_in, sums, sums_in,
    raw_sem, tags_sem, own_send, near_recv, relay_send, far_recv, relay2_send, third_recv, other_send, other_recv,
    parts_send, parts_recv, sums_send, sums_recv,
):
    gx, gy = lax.axis_index("gx"), lax.axis_index("gy")
    sizes = (lax.axis_size("gx"), lax.axis_size("gy"))
    devices = sizes[0] * sizes[1]
    me = gx * sizes[1] + gy

    d = lax.rem(me, PERIOD)
    leftward = (d >= 1) & (d <= 8)
    way = jnp.where(leftward, 1, -1)
    seat = jnp.where(leftward, d - 1, lax.rem(PERIOD - d, PERIOD))
    chain = jnp.where(leftward, RIGHT, LEFT)
    side = 1 - chain
    passes_own_back = (seat <= 2) | (seat == 7)
    has_c2 = seat <= 6
    has_c3 = seat <= 3
    has_p1 = seat <= 3
    first_seat = seat == 0
    passes_c2 = (seat >= 1) & (seat <= 4)
    lends_c2 = (seat >= 4) & (seat <= 6)
    has_other = (seat >= 1) & (seat <= 3)

    def block(offset):
        return lax.rem(me + (offset + devices), devices)

    def device(offset):
        place = block(offset)
        return (place // sizes[1], lax.rem(place, sizes[1]))

    other_core = (gx + 1 - 2 * lax.rem(gx, 2), gy)

    def raw_copy(c):
        return pltpu.make_async_copy(x_ref.at[chunk_rows(c)], raw.at[chunk_rows(c)], raw_sem.at[c])

    def tags_copy(k):
        offset = AWAY if k == X else k - REACH
        return pltpu.make_async_copy(cluster_ref.at[block(offset * way)], tags.at[k], tags_sem.at[k])

    def remote(src, dst, send_sem, recv_sem, to):
        return pltpu.make_async_remote_copy(
            src_ref=src, dst_ref=dst, send_sem=send_sem, recv_sem=recv_sem, device_id=to, device_id_type=MESH
        )

    def own_copy(which, c):
        rows = chunk_rows(c)
        return remote(
            own.at[rows], near.at[which, rows], own_send.at[which, c], near_recv.at[which, c], device(1 - 2 * which)
        )

    def relay_copy(which, c):
        rows = chunk_rows(c)
        return remote(
            near.at[which, rows], far.at[which, rows], relay_send.at[c], far_recv.at[which, c], device(1 - 2 * which)
        )

    def relay2_copy(which, c):
        rows = chunk_rows(c)
        return remote(
            far.at[which, rows], third.at[which, rows], relay2_send.at[c], third_recv.at[which, c], device(1 - 2 * which)
        )

    def other_copy(c):
        rows = chunk_rows(c)
        return remote(far.at[chain, rows], other.at[rows], other_send.at[c], other_recv.at[c], other_core)

    each_chunk(lambda c: raw_copy(c).start())
    for k in range(2 * REACH + 2):
        tags_copy(k).start()

    barrier = pltpu.get_barrier_semaphore()
    others = [k for k in range(-REACH, REACH + 1) if k != 0]
    met = [device(k) for k in others + [-AWAY, AWAY]] + [other_core]
    for to in met:
        pl.semaphore_signal(barrier, inc=1, device_id=to, device_id_type=MESH)

    def normalise(c):
        raw_copy(c).wait()

        def some(g, carry):
            rows = pl.ds(pl.multiple_of(c * CHUNK + g * 16, 16), 16)
            values = raw[rows].astype(jnp.float32)
            scale = lax.rsqrt(jnp.sum(values * values, axis=1, keepdims=True) + EPSILON)
            own[rows] = (values * scale).astype(jnp.bfloat16)
            return carry

        lax.fori_loop(0, CHUNK // 16, some, 0, unroll=2)

    def send_own(c):
        own_copy(chain, c).start()

        @pl.when(passes_own_back)
        def _():
            own_copy(side, c).start()

    normalise(0)
    pl.semaphore_wait(barrier, len(met))
    send_own(0)

    def send_step(c, carry):
        normalise(c)
        send_own(c)
        return carry

    lax.fori_loop(1, CHUNKS, send_step, 0)

    row_sums[...] = jnp.zeros_like(row_sums)
    col_sums[...] = jnp.zeros_like(col_sums)
    for k in range(2 * REACH + 2):
        tags_copy(k).wait()

    def columns_of(c):
        for kind, at in COLUMNS.items():
            columns[at, chunk_rows(c)] = across(tags[kind, pl.ds(c, 1), :])

    each_chunk(columns_of)

    refs = {S: own, C1: near.at[chain], C2: far.at[chain], C3: third.at[chain], P1: near.at[side], P2: far.at[side], X: other}

    def strip(down_kind, c, right_kind):
        down = refs[down_kind][chunk_rows(c)]
        down_tags = columns[COLUMNS[down_kind], chunk_rows(c)]
        same_block = down_kind == right_kind
        total = None
        for first in range(0, CHUNKS, 2):
            scores = scores_of(down, refs[right_kind][first * CHUNK : (first + 2) * CHUNK])
            for w in range(2):
                at = first + w
                live = down_tags == tags[right_kind, at : at + 1, :]
                if same_block:
                    place = lax.broadcasted_iota(jnp.int32, (CHUNK, CHUNK), 0) + (c - at) * CHUNK
                    live = live & (place != lax.broadcasted_iota(jnp.int32, (CHUNK, CHUNK), 1))
                cover = jnp.where(live, jnp.exp2(scores[:, w * CHUNK : (w + 1) * CHUNK] * GAIN - DROP), 0.0)
                total = cover if total is None else total + cover
                col_sums[ACROSS[right_kind], at] += jnp.sum(cover.reshape(CHUNK // 8, 8, CHUNK), axis=0)
        if not same_block:
            row_sums[DOWN[down_kind], chunk_rows(c)] += total

    each_chunk(lambda c: strip(S, c, S))

    def near_step(c):
        own_copy(chain, c).wait_recv()
        relay_copy(chain, c).start()

        @pl.when(d != 9)
        def _():
            strip(C1, c, S)

    each_chunk(near_step)

    @pl.when(has_c2)
    def _():
        def far_step(c):
            relay_copy(chain, c).wait_recv()

            @pl.when(passes_c2)
            def _():
                relay2_copy(chain, c).start()

            @pl.when(lends_c2)
            def _():
                other_copy(c).start()

            strip(C2, c, S)

        each_chunk(far_step)

    @pl.when(has_p1)
    def _():
        each_chunk(lambda c: own_copy(side, c).wait_recv())

        @pl.when(first_seat)
        def _():
            each_chunk(lambda c: strip(C1, c, P1))

        @pl.when(d == 1)
        def _():
            each_chunk(lambda c: strip(P1, c, S))

        each_chunk(lambda c: strip(C2, c, P1))

    @pl.when(has_other)
    def _():
        each_chunk(lambda c: other_copy(c).wait_recv())
        each_chunk(lambda c: strip(C2, c, X))

    @pl.when(has_c3)
    def _():
        def third_step(c):
            relay2_copy(chain, c).wait_recv()
            strip(C3, c, P1)

            @pl.when(seat == 3)
            def _():
                strip(C3, c, S)

            @pl.when(has_other & (d != 13))
            def _():
                strip(C3, c, X)

            @pl.when(first_seat)
            def _():
                relay_copy(side, c).wait_recv()
                strip(P2, c, C2)

                @pl.when(d == 1)
                def _():
                    strip(P2, c, C1)

        each_chunk(third_step)

    parts[...] = jnp.zeros_like(parts)
    for c in range(CHUNKS):
        rows = slice(c * CHUNK, (c + 1) * CHUNK)
        lane = slice(c, c + 1)
        for kind in (C1, C2, C3, P1, P2, X):
            total = None
            if kind in DOWN:
                total = jnp.sum(jnp.transpose(row_sums[DOWN[kind], rows]), axis=0, keepdims=True)
            if kind in ACROSS:
                more = jnp.sum(col_sums[ACROSS[kind], c], axis=0, keepdims=True)
                total = more if total is None else total + more
            at = PART_OFFSETS.index(AWAY if kind == X else kind - REACH)
            parts[jnp.where(leftward, at, len(PART_OFFSETS) - 1 - at), lane] = total
        own_part[lane] = jnp.sum(col_sums[ACROSS[S], c], axis=0, keepdims=True)

    def parts_copy(k):
        return remote(parts.at[k], parts_in.at[k], parts_send.at[k], parts_recv.at[k], device(PART_OFFSETS[k]))

    for k in range(len(PART_OFFSETS)):
        parts_copy(k).start()

    mine = tags[S]
    zero = jnp.zeros((CHUNKS, CHUNK), jnp.float32)

    def edge_tag(k):
        numbers = tags[REACH + k * way]
        at = numbers[CHUNKS - 1 : CHUNKS, CHUNK - 1 : CHUNK] if k < 0 else numbers[0:1, 0:1]
        return jnp.broadcast_to(at, (CHUNKS, CHUNK))

    def total_of(values):
        return jnp.broadcast_to(jnp.sum(values, keepdims=True), (CHUNKS, CHUNK))

    def own_totals(column_values):
        totals = []
        for j in range(CHUNKS):

            def add(c, acc):
                same = columns[COLUMNS[S], chunk_rows(c)] == tags[S, j : j + 1, :]
                picked = jnp.where(same, column_values(c), 0.0)
                return acc + jnp.sum(picked.reshape(CHUNK // 8, 8, CHUNK), axis=0)

            acc = lax.fori_loop(0, CHUNKS, add, jnp.zeros((8, CHUNK), jnp.float32), unroll=True)
            totals.append(jnp.sum(acc, axis=0, keepdims=True))
        return jnp.concatenate(totals, axis=0)

    counts = own_totals(lambda c: 1.0)
    for k in others:
        edge = edge_tag(k)
        many = total_of(jnp.where(tags[REACH + k * way] == edge, 1.0, 0.0))
        counts = counts + jnp.where(mine == edge, many, 0.0)

    total = own_part[...]
    for k in range(len(PART_OFFSETS)):
        parts_copy(k).wait_recv()
        total = total + parts_in[k]
    cover = jnp.where(
        total < math.exp(-SHIFT),
        jnp.log1p(jnp.minimum(total, math.exp(-SHIFT)) * math.exp(SHIFT)),
        SHIFT + jnp.log(total + math.exp(-SHIFT)),
    )
    cover_ref[...] = cover

    first_tag = jnp.broadcast_to(mine[0:1, 0:1], (CHUNKS, CHUNK))
    last_tag = jnp.broadcast_to(mine[CHUNKS - 1 : CHUNKS, CHUNK - 1 : CHUNK], (CHUNKS, CHUNK))
    sums[0] = total_of(jnp.where(mine == first_tag, cover, zero))
    sums[1] = total_of(jnp.where(mine == last_tag, cover, zero))

    def sums_copy(k):
        at = others.index(k)
        return remote(sums.at[0 if k < 0 else 1], sums_in.at[at], sums_send.at[at], sums_recv.at[at], device(k))

    for k in others:
        sums_copy(k).start()
    for c in range(CHUNKS):
        row_sums[0, c * CHUNK : (c + 1) * CHUNK] = across(cover[c : c + 1])
    cluster_sums = own_totals(lambda c: row_sums[0, chunk_rows(c)])
    for k in others:
        sums_copy(k).wait_recv()
        cluster_sums = cluster_sums + jnp.where(mine == edge_tag(-k), sums_in[others.index(k)], zero)
    relative_ref[...] = cover - cluster_sums / counts

    def sent(c):
        own_copy(chain, c).wait_send()
        relay_copy(chain, c).wait_send()

        @pl.when(passes_own_back)
        def _():
            own_copy(side, c).wait_send()

        @pl.when(passes_c2)
        def _():
            relay2_copy(chain, c).wait_send()

        @pl.when(lends_c2)
        def _():
            other_copy(c).wait_send()

    each_chunk(sent)
    for k in range(len(PART_OFFSETS)):
        parts_copy(k).wait_send()
    for k in others:
        sums_copy(k).wait_send()


def per_device(embeddings, cluster):
    rows, width = embeddings.shape
    vmem = pl.BlockSpec(memory_space=pltpu.VMEM)
    hbm = pl.BlockSpec(memory_space=pltpu.HBM)
    dma = pltpu.SemaphoreType.DMA
    small = (CHUNKS, CHUNK)
    cover, relative = pl.pallas_call(
        kernel,
        out_shape=[jax.ShapeDtypeStruct(small, jnp.float32)] * 2,
        in_specs=[hbm, hbm],
        out_specs=[vmem, vmem],
        scratch_shapes=[
            pltpu.VMEM((rows, width), jnp.bfloat16),
            pltpu.VMEM((rows, width), jnp.bfloat16),
            pltpu.VMEM((2, rows, width), jnp.bfloat16),
            pltpu.VMEM((2, rows, width), jnp.bfloat16),
            pltpu.VMEM((2, rows, width), jnp.bfloat16),
            pltpu.VMEM((rows, width), jnp.bfloat16),
            pltpu.VMEM((2 * REACH + 2, *small), jnp.int32),
            pltpu.VMEM((len(COLUMNS), rows, CHUNK), jnp.int32),
            pltpu.VMEM((len(DOWN), rows, CHUNK), jnp.float32),
            pltpu.VMEM((len(ACROSS), CHUNKS, 8, CHUNK), jnp.float32),
            pltpu.VMEM(small, jnp.float32),
            pltpu.VMEM((len(PART_OFFSETS), *small), jnp.float32),
            pltpu.VMEM((len(PART_OFFSETS), *small), jnp.float32),
            pltpu.VMEM((2, *small), jnp.float32),
            pltpu.VMEM((2 * REACH, *small), jnp.float32),
            dma((CHUNKS,)),
            dma((2 * REACH + 2,)),
            dma((2, CHUNKS)),
            dma((2, CHUNKS)),
            dma((CHUNKS,)),
            dma((2, CHUNKS)),
            dma((CHUNKS,)),
            dma((2, CHUNKS)),
            dma((CHUNKS,)),
            dma((CHUNKS,)),
            dma((len(PART_OFFSETS),)),
            dma((len(PART_OFFSETS),)),
            dma((2 * REACH,)),
            dma((2 * REACH,)),
        ],
        compiler_params=pltpu.CompilerParams(
            collective_id=0, has_side_effects=True, vmem_limit_bytes=60 << 20
        ),
        name="cover",
    )(embeddings, cluster.reshape(-1, *small))
    return cover.reshape(rows), relative.reshape(rows)


def solution(mesh):
    placed = (P(("gx", "gy"), None), P())
    return jax.shard_map(
        per_device,
        mesh=mesh,
        in_specs=placed,
        out_specs=(P(("gx", "gy")), P(("gx", "gy"))),
        check_vma=False,
    )
```

```python
import math

import jax
import jax.numpy as jnp
from jax import lax
from jax.experimental import pallas as pl
from jax.experimental.pallas import tpu as pltpu
from jax.sharding import PartitionSpec as P

MESH = pl.DeviceIdType.MESH
INVERSE_TEMP = 100.0
EPSILON = 1e-06
SHIFT = 32.0
GAIN = INVERSE_TEMP * math.log2(math.e)
DROP = SHIFT * math.log2(math.e)

ROWS = 1024
CHUNK = 128
CHUNKS = ROWS // CHUNK
LEFT, RIGHT = 0, 1
REACH = 4
PERIOD = 16

S, C1, C2, C3, P1, P2, X = REACH, REACH + 1, REACH + 2, REACH + 3, REACH - 1, REACH - 2, 2 * REACH + 1
AWAY = 6
PART_OFFSETS = [-AWAY, -3, -2, -1, 1, 2, 3, AWAY]
PAIR = 2 * CHUNK
PAIRS = ROWS // PAIR
DOWN = {S: 0, C1: 1, C2: 2, P1: 3, X: 4}
ACROSS = {S: 0, C1: 1, C2: 2, C3: 3, P1: 4, P2: 5, X: 6}


def chunk_rows(c):
    return pl.ds(pl.multiple_of(c * CHUNK, CHUNK), CHUNK)


def pair_rows(c):
    return pl.ds(pl.multiple_of(c * PAIR, PAIR), PAIR)


def across(row):
    return jnp.transpose(jnp.broadcast_to(row, (CHUNK, CHUNK)))


def scores_of(left, right):
    return lax.dot_general(left, right, (((1,), (1,)), ((), ())), preferred_element_type=jnp.float32)


def each_chunk(body):
    def step(c, carry):
        body(c)
        return carry

    lax.fori_loop(0, CHUNKS, step, 0)


def each_pair(body):
    def step(c, carry):
        body(c)
        return carry

    lax.fori_loop(0, PAIRS, step, 0)


def kernel(
    x_ref, cluster_ref, cover_ref, relative_ref,
    raw, own, near, far, third, other, tags, columns, row_sums, col_sums, own_part, parts, parts_in, sums, sums_in,
    raw_sem, tags_sem, own_send, near_recv, relay_send, far_recv, relay2_send, third_recv, other_send, other_recv,
    parts_send, parts_recv, sums_send, sums_recv,
):
    gx, gy = lax.axis_index("gx"), lax.axis_index("gy")
    sizes = (lax.axis_size("gx"), lax.axis_size("gy"))
    devices = sizes[0] * sizes[1]
    me = gx * sizes[1] + gy

    d = lax.rem(me, PERIOD)
    leftward = (d >= 1) & (d <= 8)
    way = jnp.where(leftward, 1, -1)
    seat = jnp.where(leftward, d - 1, lax.rem(PERIOD - d, PERIOD))
    chain = jnp.where(leftward, RIGHT, LEFT)
    side = 1 - chain
    passes_own_back = (seat <= 2) | (seat == 7)
    has_c2 = seat <= 6
    has_c3 = seat <= 3
    has_p1 = seat <= 3
    first_seat = seat == 0
    passes_c2 = (seat >= 1) & (seat <= 4)
    lends_c2 = (seat >= 4) & (seat <= 6)
    has_other = (seat >= 1) & (seat <= 3)

    def block(offset):
        return lax.rem(me + (offset + devices), devices)

    def device(offset):
        place = block(offset)
        return (place // sizes[1], lax.rem(place, sizes[1]))

    def chunk(n):
        return jnp.where(leftward, n, CHUNKS - 1 - n)

    def pair(n):
        return jnp.where(leftward, n, PAIRS - 1 - n)

    other_core = (gx + 1 - 2 * lax.rem(gx, 2), gy)

    def raw_copy(c):
        return pltpu.make_async_copy(x_ref.at[chunk_rows(c)], raw.at[chunk_rows(c)], raw_sem.at[c])

    def tags_copy(k):
        offset = AWAY if k == X else k - REACH
        return pltpu.make_async_copy(cluster_ref.at[block(offset * way)], tags.at[k], tags_sem.at[k])

    def remote(src, dst, send_sem, recv_sem, to):
        return pltpu.make_async_remote_copy(
            src_ref=src, dst_ref=dst, send_sem=send_sem, recv_sem=recv_sem, device_id=to, device_id_type=MESH
        )

    def own_copy(which, c):
        rows = chunk_rows(c)
        return remote(
            own.at[rows], near.at[which, rows], own_send.at[which, c], near_recv.at[which, c], device(1 - 2 * which)
        )

    def relay_copy(which, c):
        rows = chunk_rows(c)
        return remote(
            near.at[which, rows], far.at[which, rows], relay_send.at[c], far_recv.at[which, c], device(1 - 2 * which)
        )

    def relay2_copy(which, c):
        rows = chunk_rows(c)
        return remote(
            far.at[which, rows], third.at[which, rows], relay2_send.at[c], third_recv.at[which, c], device(1 - 2 * which)
        )

    def other_copy(c):
        rows = chunk_rows(c)
        return remote(far.at[chain, rows], other.at[rows], other_send.at[c], other_recv.at[c], other_core)

    each_chunk(lambda n: raw_copy(chunk(n)).start())
    for k in range(2 * REACH + 2):
        tags_copy(k).start()

    barrier = pltpu.get_barrier_semaphore()
    others = [k for k in range(-REACH, REACH + 1) if k != 0]
    met = [device(k) for k in others + [-AWAY, AWAY]] + [other_core]
    for to in met:
        pl.semaphore_signal(barrier, inc=1, device_id=to, device_id_type=MESH)

    def normalise(c):
        raw_copy(c).wait()

        def some(g, carry):
            rows = pl.ds(pl.multiple_of(c * CHUNK + g * 16, 16), 16)
            values = raw[rows].astype(jnp.float32)
            scale = lax.rsqrt(jnp.sum(values * values, axis=1, keepdims=True) + EPSILON)
            own[rows] = (values * scale).astype(jnp.bfloat16)
            return carry

        lax.fori_loop(0, CHUNK // 16, some, 0, unroll=2)

    def send_own(c):
        own_copy(chain, c).start()

        @pl.when(seat <= 2)
        def _():
            own_copy(side, c).start()

    normalise(chunk(0))
    pl.semaphore_wait(barrier, len(met))
    send_own(chunk(0))

    def send_step(n, carry):
        normalise(chunk(n))
        send_own(chunk(n))
        return carry

    lax.fori_loop(1, CHUNKS, send_step, 0)

    @pl.when(seat == 7)
    def _():
        each_chunk(lambda n: own_copy(side, chunk(CHUNKS - 1 - n)).start())

    row_sums[...] = jnp.zeros_like(row_sums)
    col_sums[...] = jnp.zeros_like(col_sums)
    for k in range(2 * REACH + 2):
        tags_copy(k).wait()

    def columns_of(c):
        for kind, at in DOWN.items():
            columns[at, chunk_rows(c)] = across(tags[kind, pl.ds(c, 1), :])

    each_chunk(columns_of)

    refs = {S: own, C1: near.at[chain], C2: far.at[chain], C3: third.at[chain], P1: near.at[side], P2: far.at[side], X: other}

    def strip(arrived, c, resident, after=None):
        late = refs[arrived][pair_rows(c)]
        same_block = arrived == resident

        def part(rows, size):
            scores = scores_of(refs[resident][rows], late)
            numbers = columns[DOWN[resident], rows]
            total = None
            for w in range(2):
                at = pl.ds(2 * c + w, 1)
                live = numbers == tags[arrived, at, :]
                if same_block:
                    place = lax.broadcasted_iota(jnp.int32, (size, CHUNK), 0) - (2 * c + w) * CHUNK
                    live = live & (place != lax.broadcasted_iota(jnp.int32, (size, CHUNK), 1))
                cover = jnp.where(live, jnp.exp2(scores[:, w * CHUNK : (w + 1) * CHUNK] * GAIN - DROP), 0.0)
                total = cover if total is None else total + cover
                col_sums[ACROSS[arrived], at] += jnp.sum(cover.reshape(size // 8, 8, CHUNK), axis=0)[None]
            if not same_block:
                row_sums[DOWN[resident], rows] += total

        if after is None:
            part(pl.ds(0, ROWS), ROWS)
        else:
            first, place_of = after

            def some(j, carry):
                part(pair_rows(place_of(j)), PAIR)
                return carry

            lax.fori_loop(first, PAIRS, some, 0)

    each_pair(lambda c: strip(S, c, S))

    def near_step(n):
        for h in range(2):
            c = chunk(2 * n + h)
            own_copy(chain, c).wait_recv()
            relay_copy(chain, c).start()

        @pl.when(d != 9)
        def _():
            strip(C1, pair(n), S)

    each_pair(near_step)

    @pl.when(has_c2)
    def _():
        def far_step(n):
            for h in range(2):
                c = chunk(2 * n + h)
                relay_copy(chain, c).wait_recv()

                @pl.when(passes_c2)
                def _():
                    relay2_copy(chain, c).start()

                @pl.when(lends_c2)
                def _():
                    other_copy(c).start()

            strip(C2, pair(n), S)

        each_pair(far_step)

    @pl.when(has_other)
    def _():
        each_chunk(lambda c: other_copy(c).wait_recv())
        each_pair(lambda n: strip(X, pair(n), C2, (n, pair)))

    @pl.when(has_p1)
    def _():
        each_chunk(lambda c: own_copy(side, c).wait_recv())

        @pl.when(first_seat)
        def _():
            each_pair(lambda c: strip(C1, c, P1))

        @pl.when(d == 1)
        def _():
            each_pair(lambda c: strip(P1, c, S))

        each_pair(lambda c: strip(C2, c, P1))

    @pl.when(has_c3)
    def _():
        def third_step(n):
            for h in range(2):
                relay2_copy(chain, chunk(2 * n + h)).wait_recv()
            strip(C3, pair(n), P1, (n, pair))

            @pl.when(seat == 3)
            def _():
                strip(C3, pair(n), S)

            @pl.when(has_other & (d != 13))
            def _():
                strip(C3, pair(n), X)

            @pl.when(first_seat)
            def _():
                for h in range(2):
                    relay_copy(side, chunk(CHUNKS - 1 - 2 * n - h)).wait_recv()
                strip(P2, pair(PAIRS - 1 - n), C2, (n, lambda j: pair(PAIRS - 1 - j)))

                @pl.when(d == 1)
                def _():
                    strip(P2, pair(PAIRS - 1 - n), C1)

        each_pair(third_step)

    ones = jnp.ones((8, CHUNK), jnp.float32)

    def sums_of(kind):
        total = None
        if kind in ACROSS:
            total = jnp.sum(col_sums[ACROSS[kind]], axis=1)
        if kind in DOWN:
            rows = lax.dot_general(
                ones, row_sums[DOWN[kind]], (((1,), (1,)), ((), ())),
                precision=lax.Precision.HIGHEST, preferred_element_type=jnp.float32,
            )
            total = total + jnp.concatenate([rows[0:1, c * CHUNK : (c + 1) * CHUNK] for c in range(CHUNKS)], axis=0)
        return total

    parts[...] = jnp.zeros_like(parts)
    for kind in (C1, C2, C3, P1, P2, X):
        at = PART_OFFSETS.index(AWAY if kind == X else kind - REACH)
        parts[jnp.where(leftward, at, len(PART_OFFSETS) - 1 - at)] = sums_of(kind)
    own_part[...] = sums_of(S)

    def parts_copy(k):
        return remote(parts.at[k], parts_in.at[k], parts_send.at[k], parts_recv.at[k], device(PART_OFFSETS[k]))

    for k in range(len(PART_OFFSETS)):
        parts_copy(k).start()

    mine = tags[S]
    zero = jnp.zeros((CHUNKS, CHUNK), jnp.float32)

    def edge_tag(k):
        numbers = tags[REACH + k * way]
        at = numbers[CHUNKS - 1 : CHUNKS, CHUNK - 1 : CHUNK] if k < 0 else numbers[0:1, 0:1]
        return jnp.broadcast_to(at, (CHUNKS, CHUNK))

    def total_of(values):
        return jnp.broadcast_to(jnp.sum(values, keepdims=True), (CHUNKS, CHUNK))

    def own_totals(column_values):
        totals = []
        for j in range(CHUNKS):

            def add(c, acc):
                same = columns[DOWN[S], chunk_rows(c)] == tags[S, j : j + 1, :]
                picked = jnp.where(same, column_values(c), 0.0)
                return acc + jnp.sum(picked.reshape(CHUNK // 8, 8, CHUNK), axis=0)

            acc = lax.fori_loop(0, CHUNKS, add, jnp.zeros((8, CHUNK), jnp.float32), unroll=True)
            totals.append(jnp.sum(acc, axis=0, keepdims=True))
        return jnp.concatenate(totals, axis=0)

    counts = own_totals(lambda c: 1.0)
    for k in others:
        edge = edge_tag(k)
        many = total_of(jnp.where(tags[REACH + k * way] == edge, 1.0, 0.0))
        counts = counts + jnp.where(mine == edge, many, 0.0)

    total = own_part[...]
    for k in range(len(PART_OFFSETS)):
        parts_copy(k).wait_recv()
        total = total + parts_in[k]
    cover = jnp.where(
        total < math.exp(-SHIFT),
        jnp.log1p(jnp.minimum(total, math.exp(-SHIFT)) * math.exp(SHIFT)),
        SHIFT + jnp.log(total + math.exp(-SHIFT)),
    )
    cover_ref[...] = cover

    first_tag = jnp.broadcast_to(mine[0:1, 0:1], (CHUNKS, CHUNK))
    last_tag = jnp.broadcast_to(mine[CHUNKS - 1 : CHUNKS, CHUNK - 1 : CHUNK], (CHUNKS, CHUNK))
    sums[0] = total_of(jnp.where(mine == first_tag, cover, zero))
    sums[1] = total_of(jnp.where(mine == last_tag, cover, zero))

    def sums_copy(k):
        at = others.index(k)
        return remote(sums.at[0 if k < 0 else 1], sums_in.at[at], sums_send.at[at], sums_recv.at[at], device(k))

    for k in others:
        sums_copy(k).start()
    for c in range(CHUNKS):
        row_sums[0, c * CHUNK : (c + 1) * CHUNK] = across(cover[c : c + 1])
    cluster_sums = own_totals(lambda c: row_sums[0, chunk_rows(c)])
    for k in others:
        sums_copy(k).wait_recv()
        cluster_sums = cluster_sums + jnp.where(mine == edge_tag(-k), sums_in[others.index(k)], zero)
    relative_ref[...] = cover - cluster_sums / counts

    def sent(c):
        own_copy(chain, c).wait_send()
        relay_copy(chain, c).wait_send()

        @pl.when(passes_own_back)
        def _():
            own_copy(side, c).wait_send()

        @pl.when(passes_c2)
        def _():
            relay2_copy(chain, c).wait_send()

        @pl.when(lends_c2)
        def _():
            other_copy(c).wait_send()

    each_chunk(sent)
    for k in range(len(PART_OFFSETS)):
        parts_copy(k).wait_send()
    for k in others:
        sums_copy(k).wait_send()


def per_device(embeddings, cluster):
    rows, width = embeddings.shape
    vmem = pl.BlockSpec(memory_space=pltpu.VMEM)
    hbm = pl.BlockSpec(memory_space=pltpu.HBM)
    dma = pltpu.SemaphoreType.DMA
    small = (CHUNKS, CHUNK)
    cover, relative = pl.pallas_call(
        kernel,
        out_shape=[jax.ShapeDtypeStruct(small, jnp.float32)] * 2,
        in_specs=[hbm, hbm],
        out_specs=[vmem, vmem],
        scratch_shapes=[
            pltpu.VMEM((rows, width), jnp.bfloat16),
            pltpu.VMEM((rows, width), jnp.bfloat16),
            pltpu.VMEM((2, rows, width), jnp.bfloat16),
            pltpu.VMEM((2, rows, width), jnp.bfloat16),
            pltpu.VMEM((2, rows, width), jnp.bfloat16),
            pltpu.VMEM((rows, width), jnp.bfloat16),
            pltpu.VMEM((2 * REACH + 2, *small), jnp.int32),
            pltpu.VMEM((len(DOWN), rows, CHUNK), jnp.int32),
            pltpu.VMEM((len(DOWN), rows, CHUNK), jnp.float32),
            pltpu.VMEM((len(ACROSS), CHUNKS, 8, CHUNK), jnp.float32),
            pltpu.VMEM(small, jnp.float32),
            pltpu.VMEM((len(PART_OFFSETS), *small), jnp.float32),
            pltpu.VMEM((len(PART_OFFSETS), *small), jnp.float32),
            pltpu.VMEM((2, *small), jnp.float32),
            pltpu.VMEM((2 * REACH, *small), jnp.float32),
            dma((CHUNKS,)),
            dma((2 * REACH + 2,)),
            dma((2, CHUNKS)),
            dma((2, CHUNKS)),
            dma((CHUNKS,)),
            dma((2, CHUNKS)),
            dma((CHUNKS,)),
            dma((2, CHUNKS)),
            dma((CHUNKS,)),
            dma((CHUNKS,)),
            dma((len(PART_OFFSETS),)),
            dma((len(PART_OFFSETS),)),
            dma((2 * REACH,)),
            dma((2 * REACH,)),
        ],
        compiler_params=pltpu.CompilerParams(
            collective_id=0, has_side_effects=True, vmem_limit_bytes=60 << 20
        ),
        name="cover",
    )(embeddings, cluster.reshape(-1, *small))
    return cover.reshape(rows), relative.reshape(rows)


def solution(mesh):
    placed = (P(("gx", "gy"), None), P())
    return jax.shard_map(
        per_device,
        mesh=mesh,
        in_specs=placed,
        out_specs=(P(("gx", "gy")), P(("gx", "gy"))),
        check_vma=False,
    )
```

```python
import math

import jax
import jax.numpy as jnp
from jax import lax
from jax.experimental import pallas as pl
from jax.experimental.pallas import tpu as pltpu
from jax.sharding import PartitionSpec as P

MESH = pl.DeviceIdType.MESH
INVERSE_TEMP = 100.0
EPSILON = 1e-06
SHIFT = 32.0
GAIN = INVERSE_TEMP * math.log2(math.e)
DROP = SHIFT * math.log2(math.e)

ROWS = 1024
CHUNK = 128
CHUNKS = ROWS // CHUNK
LEFT, RIGHT = 0, 1
REACH = 4
PERIOD = 16

S, C1, C2, C3, P1, P2, X = REACH, REACH + 1, REACH + 2, REACH + 3, REACH - 1, REACH - 2, 2 * REACH + 1
AWAY = 6
PART_OFFSETS = [-AWAY, -3, -2, -1, 1, 2, 3, AWAY]
PAIR = 2 * CHUNK
PAIRS = ROWS // PAIR
DOWN = {S: 0, C1: 1, C2: 2, P1: 3, X: 4}
ACROSS = {S: 0, C1: 1, C2: 2, C3: 3, P1: 4, P2: 5, X: 6}


def chunk_rows(c):
    return pl.ds(pl.multiple_of(c * CHUNK, CHUNK), CHUNK)


def pair_rows(c):
    return pl.ds(pl.multiple_of(c * PAIR, PAIR), PAIR)


def across(row):
    return jnp.transpose(jnp.broadcast_to(row, (CHUNK, CHUNK)))


def scores_of(left, right):
    return lax.dot_general(left, right, (((1,), (1,)), ((), ())), preferred_element_type=jnp.float32)


def each_chunk(body):
    def step(c, carry):
        body(c)
        return carry

    lax.fori_loop(0, CHUNKS, step, 0)


def each_pair(body):
    def step(c, carry):
        body(c)
        return carry

    lax.fori_loop(0, PAIRS, step, 0)


def kernel(
    x_ref, cluster_ref, cover_ref, relative_ref,
    raw, own, near, far, third, other, tags, columns, row_sums, col_sums, row_counts, own_part, parts, parts_in, sums, sums_in,
    raw_sem, tags_sem, own_send, near_recv, relay_send, far_recv, relay2_send, third_recv, other_send, other_recv,
    parts_send, parts_recv, sums_send, sums_recv,
):
    gx, gy = lax.axis_index("gx"), lax.axis_index("gy")
    sizes = (lax.axis_size("gx"), lax.axis_size("gy"))
    devices = sizes[0] * sizes[1]
    me = gx * sizes[1] + gy

    d = lax.rem(me, PERIOD)
    leftward = (d >= 1) & (d <= 8)
    way = jnp.where(leftward, 1, -1)
    seat = jnp.where(leftward, d - 1, lax.rem(PERIOD - d, PERIOD))
    chain = jnp.where(leftward, RIGHT, LEFT)
    side = 1 - chain
    passes_own_back = (seat <= 2) | (seat == 7)
    has_c2 = seat <= 6
    has_c3 = seat <= 3
    has_p1 = seat <= 3
    first_seat = seat == 0
    passes_c2 = (seat >= 1) & (seat <= 4)
    lends_c2 = (seat >= 4) & (seat <= 6)
    has_other = (seat >= 1) & (seat <= 3)

    def block(offset):
        return lax.rem(me + (offset + devices), devices)

    def device(offset):
        place = block(offset)
        return (place // sizes[1], lax.rem(place, sizes[1]))

    def chunk(n):
        return jnp.where(leftward, n, CHUNKS - 1 - n)

    def pair(n):
        return jnp.where(leftward, n, PAIRS - 1 - n)

    other_core = (gx + 1 - 2 * lax.rem(gx, 2), gy)

    def raw_copy(c):
        return pltpu.make_async_copy(x_ref.at[chunk_rows(c)], raw.at[chunk_rows(c)], raw_sem.at[c])

    def tags_copy(k):
        offset = AWAY if k == X else k - REACH
        return pltpu.make_async_copy(cluster_ref.at[block(offset * way)], tags.at[k], tags_sem.at[k])

    def remote(src, dst, send_sem, recv_sem, to):
        return pltpu.make_async_remote_copy(
            src_ref=src, dst_ref=dst, send_sem=send_sem, recv_sem=recv_sem, device_id=to, device_id_type=MESH
        )

    def own_copy(which, c):
        rows = chunk_rows(c)
        return remote(
            own.at[rows], near.at[which, rows], own_send.at[which, c], near_recv.at[which, c], device(1 - 2 * which)
        )

    def relay_copy(which, c):
        rows = chunk_rows(c)
        return remote(
            near.at[which, rows], far.at[which, rows], relay_send.at[c], far_recv.at[which, c], device(1 - 2 * which)
        )

    def relay2_copy(which, c):
        rows = chunk_rows(c)
        return remote(
            far.at[which, rows], third.at[which, rows], relay2_send.at[c], third_recv.at[which, c], device(1 - 2 * which)
        )

    def other_copy(c):
        rows = chunk_rows(c)
        return remote(far.at[chain, rows], other.at[rows], other_send.at[c], other_recv.at[c], other_core)

    each_chunk(lambda n: raw_copy(chunk(n)).start())
    for k in range(2 * REACH + 2):
        tags_copy(k).start()

    barrier = pltpu.get_barrier_semaphore()
    others = [k for k in range(-REACH, REACH + 1) if k != 0]
    met = [device(k) for k in others + [-AWAY, AWAY]] + [other_core]
    for to in met:
        pl.semaphore_signal(barrier, inc=1, device_id=to, device_id_type=MESH)

    def normalise(c):
        raw_copy(c).wait()

        def some(g, carry):
            rows = pl.ds(pl.multiple_of(c * CHUNK + g * 16, 16), 16)
            values = raw[rows].astype(jnp.float32)
            scale = lax.rsqrt(jnp.sum(values * values, axis=1, keepdims=True) + EPSILON)
            own[rows] = (values * scale).astype(jnp.bfloat16)
            return carry

        lax.fori_loop(0, CHUNK // 16, some, 0, unroll=2)

    def send_own(c):
        @pl.when(seat != 0)
        def _():
            own_copy(chain, c).start()

    def send_late(n):
        for h in range(2):
            own_copy(side, chunk(CHUNKS - 1 - 2 * n - h)).start()

    normalise(chunk(0))
    pl.semaphore_wait(barrier, len(met))
    send_own(chunk(0))

    def send_step(n, carry):
        normalise(chunk(n))
        send_own(chunk(n))
        return carry

    lax.fori_loop(1, CHUNKS, send_step, 0)

    @pl.when(seat == 7)
    def _():
        each_pair(send_late)

    row_sums[...] = jnp.zeros_like(row_sums)
    col_sums[...] = jnp.zeros_like(col_sums)
    for k in range(2 * REACH + 2):
        tags_copy(k).wait()

    def columns_of(c):
        for kind, at in DOWN.items():
            columns[at, chunk_rows(c)] = across(tags[kind, pl.ds(c, 1), :])

    each_chunk(columns_of)

    mine = tags[S]
    zero = jnp.zeros((CHUNKS, CHUNK), jnp.float32)

    def edge_tag(k):
        numbers = tags[REACH + k * way]
        at = numbers[CHUNKS - 1 : CHUNKS, CHUNK - 1 : CHUNK] if k < 0 else numbers[0:1, 0:1]
        return jnp.broadcast_to(at, (CHUNKS, CHUNK))

    def total_of(values):
        return jnp.broadcast_to(jnp.sum(values, keepdims=True), (CHUNKS, CHUNK))

    def own_totals(column_values):
        totals = []
        for j in range(CHUNKS):

            def add(c, acc):
                same = columns[DOWN[S], chunk_rows(c)] == tags[S, j : j + 1, :]
                picked = jnp.where(same, column_values(c), 0.0)
                return acc + jnp.sum(picked.reshape(CHUNK // 8, 8, CHUNK), axis=0)

            acc = lax.fori_loop(0, CHUNKS, add, jnp.zeros((8, CHUNK), jnp.float32), unroll=True)
            totals.append(jnp.sum(acc, axis=0, keepdims=True))
        return jnp.concatenate(totals, axis=0)

    counts = own_totals(lambda c: 1.0)
    for k in others:
        edge = edge_tag(k)
        many = total_of(jnp.where(tags[REACH + k * way] == edge, 1.0, 0.0))
        counts = counts + jnp.where(mine == edge, many, 0.0)
    row_counts[...] = counts

    refs = {S: own, C1: near.at[chain], C2: far.at[chain], C3: third.at[chain], P1: near.at[side], P2: far.at[side], X: other}

    def piece(arrived, c, resident, rows, size):
        scores = scores_of(refs[resident][rows], refs[arrived][pair_rows(c)])
        numbers = columns[DOWN[resident], rows]
        total = None
        for w in range(2):
            at = pl.ds(2 * c + w, 1)
            live = numbers == tags[arrived, at, :]
            if arrived == resident:
                place = lax.broadcasted_iota(jnp.int32, (size, CHUNK), 0) - (2 * c + w) * CHUNK
                live = live & (place != lax.broadcasted_iota(jnp.int32, (size, CHUNK), 1))
            cover = jnp.where(live, jnp.exp2(scores[:, w * CHUNK : (w + 1) * CHUNK] * GAIN - DROP), 0.0)
            total = cover if total is None else total + cover
            col_sums[ACROSS[arrived], at] += jnp.sum(cover.reshape(size // 8, 8, CHUNK), axis=0)[None]
        if arrived != resident:
            row_sums[DOWN[resident], rows] += total

    def strip(arrived, c, resident):
        piece(arrived, c, resident, pl.ds(0, ROWS), ROWS)

    def pieces(first, last, arrived, c_of, resident, r_of):
        def some(j, carry):
            piece(arrived, c_of(j), resident, pair_rows(r_of(j)), PAIR)
            return carry

        lax.fori_loop(first, last, some, 0)

    each_pair(lambda c: strip(S, c, S))

    def near_step(n):
        for h in range(2):
            c = chunk(2 * n + h)
            own_copy(chain, c).wait_recv()
            relay_copy(chain, c).start()

            @pl.when(seat == 0)
            def _():
                own_copy(chain, c).start()

        @pl.when(d != 9)
        def _():
            strip(C1, pair(n), S)

    each_pair(near_step)

    @pl.when(has_c2)
    def _():
        def far_step(n):
            for h in range(2):
                c = chunk(2 * n + h)
                relay_copy(chain, c).wait_recv()

                @pl.when(passes_c2)
                def _():
                    relay2_copy(chain, c).start()

                @pl.when(lends_c2)
                def _():
                    other_copy(c).start()

            @pl.when((seat <= 2) & (n >= 2))
            def _():
                send_late(n - 2)

            strip(C2, pair(n), S)

        each_pair(far_step)

    @pl.when(seat <= 2)
    def _():
        send_late(2)
        send_late(3)

    @pl.when(has_other)
    def _():
        def other_step(n):
            last = PAIRS - 1 - n
            for h in range(2):
                other_copy(chunk(2 * last + 1 - h)).wait_recv()
            pieces(last, PAIRS, X, lambda j: pair(last), C2, pair)

        each_pair(other_step)

    def side_step(n):
        last = PAIRS - 1 - n
        for h in range(2):
            own_copy(side, chunk(2 * last + 1 - h)).wait_recv()
        strip(P1, pair(last), C2)

    @pl.when(first_seat)
    def _():
        def first_step(n):
            side_step(n)
            strip(P1, pair(PAIRS - 1 - n), C1)

            @pl.when(d == 1)
            def _():
                strip(P1, pair(PAIRS - 1 - n), S)

        each_pair(first_step)

    @pl.when(has_c3)
    def _():
        def third_step(n):
            last = PAIRS - 1 - n
            for h in range(2):
                relay2_copy(chain, chunk(2 * n + h)).wait_recv()

            @pl.when(seat == 3)
            def _():
                strip(C3, pair(n), S)

            @pl.when(has_other & (d != 13))
            def _():
                strip(C3, pair(n), X)

            @pl.when(has_other)
            def _():
                side_step(n)

            pieces(jnp.maximum(n, last), PAIRS, C3, lambda j: pair(n), P1, pair)
            pieces(0, jnp.minimum(n, last + 1), C3, pair, P1, lambda j: pair(last))

            @pl.when(first_seat)
            def _():
                for h in range(2):
                    relay_copy(side, chunk(2 * last + 1 - h)).wait_recv()
                pieces(n, PAIRS, P2, lambda j: pair(last), C2, lambda j: pair(PAIRS - 1 - j))

                @pl.when(d == 1)
                def _():
                    strip(P2, pair(last), C1)

        each_pair(third_step)

    def sums_of(kind):
        total = None
        if kind in ACROSS:
            total = jnp.sum(col_sums[ACROSS[kind]], axis=1)
        if kind in DOWN:
            rows = [row_sums[DOWN[kind], c * CHUNK : (c + 1) * CHUNK] for c in range(CHUNKS)]
            total = total + jnp.concatenate([jnp.sum(jnp.transpose(r), axis=0, keepdims=True) for r in rows], axis=0)
        return total

    parts[...] = jnp.zeros_like(parts)
    for kind in (C1, C2, C3, P1, P2, X):
        at = PART_OFFSETS.index(AWAY if kind == X else kind - REACH)
        parts[jnp.where(leftward, at, len(PART_OFFSETS) - 1 - at)] = sums_of(kind)
    own_part[...] = sums_of(S)

    def parts_copy(k):
        return remote(parts.at[k], parts_in.at[k], parts_send.at[k], parts_recv.at[k], device(PART_OFFSETS[k]))

    for k in range(len(PART_OFFSETS)):
        parts_copy(k).start()

    total = own_part[...]
    for k in range(len(PART_OFFSETS)):
        parts_copy(k).wait_recv()
        total = total + parts_in[k]
    cover = jnp.where(
        total < math.exp(-SHIFT),
        jnp.log1p(jnp.minimum(total, math.exp(-SHIFT)) * math.exp(SHIFT)),
        SHIFT + jnp.log(total + math.exp(-SHIFT)),
    )
    cover_ref[...] = cover

    first_tag = jnp.broadcast_to(mine[0:1, 0:1], (CHUNKS, CHUNK))
    last_tag = jnp.broadcast_to(mine[CHUNKS - 1 : CHUNKS, CHUNK - 1 : CHUNK], (CHUNKS, CHUNK))
    sums[0] = total_of(jnp.where(mine == first_tag, cover, zero))
    sums[1] = total_of(jnp.where(mine == last_tag, cover, zero))

    def sums_copy(k):
        at = others.index(k)
        return remote(sums.at[0 if k < 0 else 1], sums_in.at[at], sums_send.at[at], sums_recv.at[at], device(k))

    for k in others:
        sums_copy(k).start()
    for c in range(CHUNKS):
        row_sums[0, c * CHUNK : (c + 1) * CHUNK] = across(cover[c : c + 1])
    cluster_sums = own_totals(lambda c: row_sums[0, chunk_rows(c)])
    for k in others:
        sums_copy(k).wait_recv()
        cluster_sums = cluster_sums + jnp.where(mine == edge_tag(-k), sums_in[others.index(k)], zero)
    relative_ref[...] = cover - cluster_sums / row_counts[...]

    def sent(c):
        own_copy(chain, c).wait_send()
        relay_copy(chain, c).wait_send()

        @pl.when(passes_own_back)
        def _():
            own_copy(side, c).wait_send()

        @pl.when(passes_c2)
        def _():
            relay2_copy(chain, c).wait_send()

        @pl.when(lends_c2)
        def _():
            other_copy(c).wait_send()

    each_chunk(sent)
    for k in range(len(PART_OFFSETS)):
        parts_copy(k).wait_send()
    for k in others:
        sums_copy(k).wait_send()


def per_device(embeddings, cluster):
    rows, width = embeddings.shape
    vmem = pl.BlockSpec(memory_space=pltpu.VMEM)
    hbm = pl.BlockSpec(memory_space=pltpu.HBM)
    dma = pltpu.SemaphoreType.DMA
    small = (CHUNKS, CHUNK)
    cover, relative = pl.pallas_call(
        kernel,
        out_shape=[jax.ShapeDtypeStruct(small, jnp.float32)] * 2,
        in_specs=[hbm, hbm],
        out_specs=[vmem, vmem],
        scratch_shapes=[
            pltpu.VMEM((rows, width), jnp.bfloat16),
            pltpu.VMEM((rows, width), jnp.bfloat16),
            pltpu.VMEM((2, rows, width), jnp.bfloat16),
            pltpu.VMEM((2, rows, width), jnp.bfloat16),
            pltpu.VMEM((2, rows, width), jnp.bfloat16),
            pltpu.VMEM((rows, width), jnp.bfloat16),
            pltpu.VMEM((2 * REACH + 2, *small), jnp.int32),
            pltpu.VMEM((len(DOWN), rows, CHUNK), jnp.int32),
            pltpu.VMEM((len(DOWN), rows, CHUNK), jnp.float32),
            pltpu.VMEM((len(ACROSS), CHUNKS, 8, CHUNK), jnp.float32),
            pltpu.VMEM(small, jnp.float32),
            pltpu.VMEM(small, jnp.float32),
            pltpu.VMEM((len(PART_OFFSETS), *small), jnp.float32),
            pltpu.VMEM((len(PART_OFFSETS), *small), jnp.float32),
            pltpu.VMEM((2, *small), jnp.float32),
            pltpu.VMEM((2 * REACH, *small), jnp.float32),
            dma((CHUNKS,)),
            dma((2 * REACH + 2,)),
            dma((2, CHUNKS)),
            dma((2, CHUNKS)),
            dma((CHUNKS,)),
            dma((2, CHUNKS)),
            dma((CHUNKS,)),
            dma((2, CHUNKS)),
            dma((CHUNKS,)),
            dma((CHUNKS,)),
            dma((len(PART_OFFSETS),)),
            dma((len(PART_OFFSETS),)),
            dma((2 * REACH,)),
            dma((2 * REACH,)),
        ],
        compiler_params=pltpu.CompilerParams(
            collective_id=0, has_side_effects=True, vmem_limit_bytes=60 << 20
        ),
        name="cover",
    )(embeddings, cluster.reshape(-1, *small))
    return cover.reshape(rows), relative.reshape(rows)


def solution(mesh):
    placed = (P(("gx", "gy"), None), P())
    return jax.shard_map(
        per_device,
        mesh=mesh,
        in_specs=placed,
        out_specs=(P(("gx", "gy")), P(("gx", "gy"))),
        check_vma=False,
    )
```

```python
import math

import jax
import jax.numpy as jnp
from jax import lax
from jax.experimental import pallas as pl
from jax.experimental.pallas import tpu as pltpu
from jax.sharding import PartitionSpec as P

MESH = pl.DeviceIdType.MESH
INVERSE_TEMP = 100.0
EPSILON = 1e-06
SHIFT = 32.0
GAIN = INVERSE_TEMP * math.log2(math.e)
DROP = SHIFT * math.log2(math.e)

ROWS = 1024
CHUNK = 128
CHUNKS = ROWS // CHUNK
LEFT, RIGHT = 0, 1
REACH = 4
PERIOD = 16

S, C1, C2, C3, P1, P2, X = REACH, REACH + 1, REACH + 2, REACH + 3, REACH - 1, REACH - 2, 2 * REACH + 1
AWAY = 6
PART_OFFSETS = [-AWAY, -3, -2, -1, 1, 2, 3, AWAY]
PAIR = 2 * CHUNK
PAIRS = ROWS // PAIR
DOWN = {S: 0, C1: 1, C2: 2, P1: 3, X: 4}
ACROSS = {S: 0, C1: 1, C2: 2, C3: 3, P1: 4, P2: 5, X: 6}


def chunk_rows(c):
    return pl.ds(pl.multiple_of(c * CHUNK, CHUNK), CHUNK)


def pair_rows(c):
    return pl.ds(pl.multiple_of(c * PAIR, PAIR), PAIR)


def across(row):
    return jnp.transpose(jnp.broadcast_to(row, (CHUNK, CHUNK)))


def scores_of(left, right):
    return lax.dot_general(left, right, (((1,), (1,)), ((), ())), preferred_element_type=jnp.float32)


def each_chunk(body):
    def step(c, carry):
        body(c)
        return carry

    lax.fori_loop(0, CHUNKS, step, 0)


def each_pair(body):
    def step(c, carry):
        body(c)
        return carry

    lax.fori_loop(0, PAIRS, step, 0)


def kernel(
    x_ref, cluster_ref, cover_ref, relative_ref,
    raw, own, near, far, third, other, tags, columns, row_sums, col_sums, row_counts, masks, own_part, parts, parts_in, sums, sums_in,
    raw_sem, tags_sem, own_send, near_recv, relay_send, far_recv, relay2_send, third_recv, other_send, other_recv,
    parts_send, parts_recv, sums_send, sums_recv,
):
    gx, gy = lax.axis_index("gx"), lax.axis_index("gy")
    sizes = (lax.axis_size("gx"), lax.axis_size("gy"))
    devices = sizes[0] * sizes[1]
    me = gx * sizes[1] + gy

    d = lax.rem(me, PERIOD)
    leftward = (d >= 1) & (d <= 8)
    way = jnp.where(leftward, 1, -1)
    seat = jnp.where(leftward, d - 1, lax.rem(PERIOD - d, PERIOD))
    chain = jnp.where(leftward, RIGHT, LEFT)
    side = 1 - chain
    passes_own_back = (seat <= 2) | (seat == 7)
    has_c2 = seat <= 6
    has_c3 = seat <= 3
    has_p1 = seat <= 3
    first_seat = seat == 0
    passes_c2 = (seat >= 1) & (seat <= 4)
    lends_c2 = (seat >= 4) & (seat <= 6)
    has_other = (seat >= 1) & (seat <= 3)

    def block(offset):
        return lax.rem(me + (offset + devices), devices)

    def device(offset):
        place = block(offset)
        return (place // sizes[1], lax.rem(place, sizes[1]))

    def chunk(n):
        return jnp.where(leftward, n, CHUNKS - 1 - n)

    def pair(n):
        return jnp.where(leftward, n, PAIRS - 1 - n)

    other_core = (gx + 1 - 2 * lax.rem(gx, 2), gy)

    def raw_copy(c):
        return pltpu.make_async_copy(x_ref.at[chunk_rows(c)], raw.at[chunk_rows(c)], raw_sem.at[c])

    def tags_copy(k):
        offset = AWAY if k == X else k - REACH
        return pltpu.make_async_copy(cluster_ref.at[block(offset * way)], tags.at[k], tags_sem.at[k])

    def remote(src, dst, send_sem, recv_sem, to):
        return pltpu.make_async_remote_copy(
            src_ref=src, dst_ref=dst, send_sem=send_sem, recv_sem=recv_sem, device_id=to, device_id_type=MESH
        )

    def own_copy(which, c):
        rows = chunk_rows(c)
        return remote(
            own.at[rows], near.at[which, rows], own_send.at[which, c], near_recv.at[which, c], device(1 - 2 * which)
        )

    def relay_copy(which, c):
        rows = chunk_rows(c)
        return remote(
            near.at[which, rows], far.at[which, rows], relay_send.at[c], far_recv.at[which, c], device(1 - 2 * which)
        )

    def relay2_copy(which, c):
        rows = chunk_rows(c)
        return remote(
            far.at[which, rows], third.at[which, rows], relay2_send.at[c], third_recv.at[which, c], device(1 - 2 * which)
        )

    def other_copy(c):
        rows = chunk_rows(c)
        return remote(far.at[chain, rows], other.at[rows], other_send.at[c], other_recv.at[c], other_core)

    each_chunk(lambda n: raw_copy(chunk(n)).start())
    for k in range(2 * REACH + 2):
        tags_copy(k).start()

    barrier = pltpu.get_barrier_semaphore()
    others = [k for k in range(-REACH, REACH + 1) if k != 0]
    met = [device(k) for k in others + [-AWAY, AWAY]] + [other_core]
    for to in met:
        pl.semaphore_signal(barrier, inc=1, device_id=to, device_id_type=MESH)

    def normalise(c):
        raw_copy(c).wait()

        def some(g, carry):
            rows = pl.ds(pl.multiple_of(c * CHUNK + g * 16, 16), 16)
            values = raw[rows].astype(jnp.float32)
            scale = lax.rsqrt(jnp.sum(values * values, axis=1, keepdims=True) + EPSILON)
            own[rows] = (values * scale).astype(jnp.bfloat16)
            return carry

        lax.fori_loop(0, CHUNK // 16, some, 0, unroll=2)

    def send_late(n):
        for h in range(2):
            own_copy(side, chunk(CHUNKS - 1 - 2 * n - h)).start()

    normalise(chunk(0))
    pl.semaphore_wait(barrier, len(met))
    own_copy(chain, chunk(0)).start()

    def send_step(n, carry):
        normalise(chunk(n))
        own_copy(chain, chunk(n)).start()
        return carry

    lax.fori_loop(1, CHUNKS, send_step, 0)

    @pl.when(seat == 7)
    def _():
        each_pair(send_late)

    row_sums[...] = jnp.zeros_like(row_sums)
    col_sums[...] = jnp.zeros_like(col_sums)
    for k in range(2 * REACH + 2):
        tags_copy(k).wait()

    def columns_of(c):
        for kind, at in DOWN.items():
            columns[at, chunk_rows(c)] = across(tags[kind, pl.ds(c, 1), :])

    each_chunk(columns_of)

    mine = tags[S]

    def edge_tag(k):
        numbers = tags[REACH + k * way]
        at = numbers[CHUNKS - 1 : CHUNKS, CHUNK - 1 : CHUNK] if k < 0 else numbers[0:1, 0:1]
        return jnp.broadcast_to(at, (CHUNKS, CHUNK))

    def total_of(values):
        return jnp.broadcast_to(jnp.sum(values, keepdims=True), (CHUNKS, CHUNK))

    def own_totals(column_values):
        totals = []
        for j in range(CHUNKS):

            def add(c, acc):
                same = columns[DOWN[S], chunk_rows(c)] == tags[S, j : j + 1, :]
                picked = jnp.where(same, column_values(c), 0.0)
                return acc + jnp.sum(picked.reshape(CHUNK // 8, 8, CHUNK), axis=0)

            acc = lax.fori_loop(0, CHUNKS, add, jnp.zeros((8, CHUNK), jnp.float32), unroll=True)
            totals.append(jnp.sum(acc, axis=0, keepdims=True))
        return jnp.concatenate(totals, axis=0)

    counts = own_totals(lambda c: 1.0)
    for k in others:
        edge = edge_tag(k)
        many = total_of(jnp.where(tags[REACH + k * way] == edge, 1.0, 0.0))
        counts = counts + jnp.where(mine == edge, many, 0.0)
        masks[others.index(k)] = jnp.where(mine == edge, 1.0, 0.0)
    row_counts[...] = counts
    first_tag = jnp.broadcast_to(mine[0:1, 0:1], (CHUNKS, CHUNK))
    last_tag = jnp.broadcast_to(mine[CHUNKS - 1 : CHUNKS, CHUNK - 1 : CHUNK], (CHUNKS, CHUNK))
    masks[len(others)] = jnp.where(mine == first_tag, 1.0, 0.0)
    masks[len(others) + 1] = jnp.where(mine == last_tag, 1.0, 0.0)

    refs = {S: own, C1: near.at[chain], C2: far.at[chain], C3: third.at[chain], P1: near.at[side], P2: far.at[side], X: other}

    def piece(arrived, c, resident, rows, size):
        scores = scores_of(refs[resident][rows], refs[arrived][pair_rows(c)])
        numbers = columns[DOWN[resident], rows]
        total = None
        for w in range(2):
            at = pl.ds(2 * c + w, 1)
            live = numbers == tags[arrived, at, :]
            if arrived == resident:
                place = lax.broadcasted_iota(jnp.int32, (size, CHUNK), 0) - (2 * c + w) * CHUNK
                live = live & (place != lax.broadcasted_iota(jnp.int32, (size, CHUNK), 1))
            cover = jnp.where(live, jnp.exp2(scores[:, w * CHUNK : (w + 1) * CHUNK] * GAIN - DROP), 0.0)
            total = cover if total is None else total + cover
            col_sums[ACROSS[arrived], at] += jnp.sum(cover.reshape(size // 8, 8, CHUNK), axis=0)[None]
        if arrived != resident:
            row_sums[DOWN[resident], rows] += total

    def strip(arrived, c, resident):
        piece(arrived, c, resident, pl.ds(0, ROWS), ROWS)

    def pieces(first, last, arrived, c_of, resident, r_of):
        def some(j, carry):
            piece(arrived, c_of(j), resident, pair_rows(r_of(j)), PAIR)
            return carry

        lax.fori_loop(first, last, some, 0)

    each_pair(lambda c: strip(S, c, S))

    def near_step(n):
        for h in range(2):
            c = chunk(2 * n + h)
            own_copy(chain, c).wait_recv()

            @pl.when(seat != 0)
            def _():
                relay_copy(chain, c).start()

        @pl.when(d != 9)
        def _():
            strip(C1, pair(n), S)

    each_pair(near_step)

    @pl.when(has_c2)
    def _():
        def far_step(n):
            for h in range(2):
                c = chunk(2 * n + h)
                relay_copy(chain, c).wait_recv()

                @pl.when(seat == 0)
                def _():
                    relay_copy(chain, c).start()

                @pl.when(passes_c2)
                def _():
                    relay2_copy(chain, c).start()

                @pl.when(lends_c2)
                def _():
                    other_copy(c).start()

            @pl.when((seat <= 2) & (n >= 2))
            def _():
                send_late(n - 2)

            strip(C2, pair(n), S)

        each_pair(far_step)

    @pl.when(seat <= 2)
    def _():
        send_late(2)
        send_late(3)

    @pl.when(has_other)
    def _():
        def other_step(n):
            last = PAIRS - 1 - n
            for h in range(2):
                other_copy(chunk(2 * last + 1 - h)).wait_recv()
            pieces(last, PAIRS, X, lambda j: pair(last), C2, pair)

        each_pair(other_step)

    def side_step(n):
        last = PAIRS - 1 - n
        for h in range(2):
            own_copy(side, chunk(2 * last + 1 - h)).wait_recv()
        strip(P1, pair(last), C2)

    @pl.when(first_seat)
    def _():
        def first_step(n):
            side_step(n)
            strip(P1, pair(PAIRS - 1 - n), C1)

            @pl.when(d == 1)
            def _():
                strip(P1, pair(PAIRS - 1 - n), S)

        each_pair(first_step)

    @pl.when(has_c3)
    def _():
        def third_step(n):
            last = PAIRS - 1 - n
            for h in range(2):
                relay2_copy(chain, chunk(2 * n + h)).wait_recv()

            @pl.when(seat == 3)
            def _():
                strip(C3, pair(n), S)

            @pl.when(has_other & (d != 13))
            def _():
                strip(C3, pair(n), X)

            @pl.when(has_other)
            def _():
                side_step(n)

            pieces(jnp.maximum(n, last), PAIRS, C3, lambda j: pair(n), P1, pair)
            pieces(0, jnp.minimum(n, last + 1), C3, pair, P1, lambda j: pair(last))

            @pl.when(first_seat)
            def _():
                for h in range(2):
                    relay_copy(side, chunk(2 * last + 1 - h)).wait_recv()
                pieces(n, PAIRS, P2, lambda j: pair(last), C2, lambda j: pair(PAIRS - 1 - j))

                @pl.when(d == 1)
                def _():
                    strip(P2, pair(last), C1)

        each_pair(third_step)

    def sums_of(kind):
        total = None
        if kind in ACROSS:
            total = jnp.sum(col_sums[ACROSS[kind]], axis=1)
        if kind in DOWN:
            rows = [row_sums[DOWN[kind], c * CHUNK : (c + 1) * CHUNK] for c in range(CHUNKS)]
            total = total + jnp.concatenate([jnp.sum(jnp.transpose(r), axis=0, keepdims=True) for r in rows], axis=0)
        return total

    parts[...] = jnp.zeros_like(parts)
    for kind in (C1, C2, C3, P1, P2, X):
        at = PART_OFFSETS.index(AWAY if kind == X else kind - REACH)
        parts[jnp.where(leftward, at, len(PART_OFFSETS) - 1 - at)] = sums_of(kind)
    own_part[...] = sums_of(S)

    def parts_copy(k):
        return remote(parts.at[k], parts_in.at[k], parts_send.at[k], parts_recv.at[k], device(PART_OFFSETS[k]))

    for k in range(len(PART_OFFSETS)):
        parts_copy(k).start()

    total = own_part[...]
    for k in range(len(PART_OFFSETS)):
        parts_copy(k).wait_recv()
        total = total + parts_in[k]
    cover = jnp.where(
        total < math.exp(-SHIFT),
        jnp.log1p(jnp.minimum(total, math.exp(-SHIFT)) * math.exp(SHIFT)),
        SHIFT + jnp.log(total + math.exp(-SHIFT)),
    )
    cover_ref[...] = cover

    for k in range(2):
        sums[k] = total_of(masks[len(others) + k] * cover)

    def sums_copy(k):
        at = others.index(k)
        return remote(sums.at[0 if k < 0 else 1], sums_in.at[at], sums_send.at[at], sums_recv.at[at], device(k))

    for k in others:
        sums_copy(k).start()
    for c in range(CHUNKS):
        row_sums[0, c * CHUNK : (c + 1) * CHUNK] = across(cover[c : c + 1])
    cluster_sums = own_totals(lambda c: row_sums[0, chunk_rows(c)])
    for k in others:
        sums_copy(k).wait_recv()
        cluster_sums = cluster_sums + masks[others.index(-k)] * sums_in[others.index(k)]
    relative_ref[...] = cover - cluster_sums / row_counts[...]

    def sent(c):
        own_copy(chain, c).wait_send()
        relay_copy(chain, c).wait_send()

        @pl.when(passes_own_back)
        def _():
            own_copy(side, c).wait_send()

        @pl.when(passes_c2)
        def _():
            relay2_copy(chain, c).wait_send()

        @pl.when(lends_c2)
        def _():
            other_copy(c).wait_send()

    each_chunk(sent)
    for k in range(len(PART_OFFSETS)):
        parts_copy(k).wait_send()
    for k in others:
        sums_copy(k).wait_send()


def per_device(embeddings, cluster):
    rows, width = embeddings.shape
    vmem = pl.BlockSpec(memory_space=pltpu.VMEM)
    hbm = pl.BlockSpec(memory_space=pltpu.HBM)
    dma = pltpu.SemaphoreType.DMA
    small = (CHUNKS, CHUNK)
    cover, relative = pl.pallas_call(
        kernel,
        out_shape=[jax.ShapeDtypeStruct(small, jnp.float32)] * 2,
        in_specs=[hbm, hbm],
        out_specs=[vmem, vmem],
        scratch_shapes=[
            pltpu.VMEM((rows, width), jnp.bfloat16),
            pltpu.VMEM((rows, width), jnp.bfloat16),
            pltpu.VMEM((2, rows, width), jnp.bfloat16),
            pltpu.VMEM((2, rows, width), jnp.bfloat16),
            pltpu.VMEM((2, rows, width), jnp.bfloat16),
            pltpu.VMEM((rows, width), jnp.bfloat16),
            pltpu.VMEM((2 * REACH + 2, *small), jnp.int32),
            pltpu.VMEM((len(DOWN), rows, CHUNK), jnp.int32),
            pltpu.VMEM((len(DOWN), rows, CHUNK), jnp.float32),
            pltpu.VMEM((len(ACROSS), CHUNKS, 8, CHUNK), jnp.float32),
            pltpu.VMEM(small, jnp.float32),
            pltpu.VMEM((2 * REACH + 2, *small), jnp.float32),
            pltpu.VMEM(small, jnp.float32),
            pltpu.VMEM((len(PART_OFFSETS), *small), jnp.float32),
            pltpu.VMEM((len(PART_OFFSETS), *small), jnp.float32),
            pltpu.VMEM((2, *small), jnp.float32),
            pltpu.VMEM((2 * REACH, *small), jnp.float32),
            dma((CHUNKS,)),
            dma((2 * REACH + 2,)),
            dma((2, CHUNKS)),
            dma((2, CHUNKS)),
            dma((CHUNKS,)),
            dma((2, CHUNKS)),
            dma((CHUNKS,)),
            dma((2, CHUNKS)),
            dma((CHUNKS,)),
            dma((CHUNKS,)),
            dma((len(PART_OFFSETS),)),
            dma((len(PART_OFFSETS),)),
            dma((2 * REACH,)),
            dma((2 * REACH,)),
        ],
        compiler_params=pltpu.CompilerParams(
            collective_id=0, has_side_effects=True, vmem_limit_bytes=60 << 20
        ),
        name="cover",
    )(embeddings, cluster.reshape(-1, *small))
    return cover.reshape(rows), relative.reshape(rows)


def solution(mesh):
    placed = (P(("gx", "gy"), None), P())
    return jax.shard_map(
        per_device,
        mesh=mesh,
        in_specs=placed,
        out_specs=(P(("gx", "gy")), P(("gx", "gy"))),
        check_vma=False,
    )
```

```python
import math

import jax
import jax.numpy as jnp
from jax import lax
from jax.experimental import pallas as pl
from jax.experimental.pallas import tpu as pltpu
from jax.sharding import PartitionSpec as P

MESH = pl.DeviceIdType.MESH
INVERSE_TEMP = 100.0
EPSILON = 1e-06
SHIFT = 32.0
GAIN = INVERSE_TEMP * math.log2(math.e)
DROP = SHIFT * math.log2(math.e)

ROWS = 1024
CHUNK = 128
CHUNKS = ROWS // CHUNK
LEFT, RIGHT = 0, 1
REACH = 4
PERIOD = 16

S, C1, C2, C3, P1, P2, X = REACH, REACH + 1, REACH + 2, REACH + 3, REACH - 1, REACH - 2, 2 * REACH + 1
AWAY = 6
PART_OFFSETS = [-AWAY, -3, -2, -1, 1, 2, 3, AWAY]
PAIR = 2 * CHUNK
PAIRS = ROWS // PAIR
DOWN = {S: 0, C1: 1, C2: 2, P1: 3, X: 4}
ACROSS = {S: 0, C1: 1, C2: 2, C3: 3, P1: 4, P2: 5, X: 6}


def chunk_rows(c):
    return pl.ds(pl.multiple_of(c * CHUNK, CHUNK), CHUNK)


def pair_rows(c):
    return pl.ds(pl.multiple_of(c * PAIR, PAIR), PAIR)


def across(row):
    return jnp.transpose(jnp.broadcast_to(row, (CHUNK, CHUNK)))


def scores_of(left, right):
    return lax.dot_general(left, right, (((1,), (1,)), ((), ())), preferred_element_type=jnp.float32)


def each_chunk(body):
    def step(c, carry):
        body(c)
        return carry

    lax.fori_loop(0, CHUNKS, step, 0)


def each_pair(body):
    def step(c, carry):
        body(c)
        return carry

    lax.fori_loop(0, PAIRS, step, 0)


def kernel(
    x_ref, cluster_ref, cover_ref, relative_ref,
    raw, own, near, far, third, other, tags, columns, row_sums, col_sums, row_counts, masks, own_part, parts, parts_in, sums, sums_in,
    raw_sem, tags_sem, own_send, near_recv, relay_send, far_recv, relay2_send, third_recv, other_send, other_recv,
    parts_send, parts_recv, sums_send, sums_recv,
):
    gx, gy = lax.axis_index("gx"), lax.axis_index("gy")
    sizes = (lax.axis_size("gx"), lax.axis_size("gy"))
    devices = sizes[0] * sizes[1]
    me = gx * sizes[1] + gy

    d = lax.rem(me, PERIOD)
    leftward = (d >= 1) & (d <= 8)
    way = jnp.where(leftward, 1, -1)
    seat = jnp.where(leftward, d - 1, lax.rem(PERIOD - d, PERIOD))
    chain = jnp.where(leftward, RIGHT, LEFT)
    side = 1 - chain
    passes_own_back = (seat <= 2) | (seat == 7)
    has_c2 = seat <= 6
    has_c3 = seat <= 3
    has_p1 = seat <= 3
    first_seat = seat == 0
    passes_c2 = (seat >= 1) & (seat <= 4)
    lends_c2 = (seat >= 4) & (seat <= 6)
    has_other = (seat >= 1) & (seat <= 3)

    def block(offset):
        return lax.rem(me + (offset + devices), devices)

    def device(offset):
        place = block(offset)
        return (place // sizes[1], lax.rem(place, sizes[1]))

    def chunk(n):
        return jnp.where(leftward, n, CHUNKS - 1 - n)

    def pair(n):
        return jnp.where(leftward, n, PAIRS - 1 - n)

    other_core = (gx + 1 - 2 * lax.rem(gx, 2), gy)

    def raw_copy(c):
        return pltpu.make_async_copy(x_ref.at[chunk_rows(c)], raw.at[chunk_rows(c)], raw_sem.at[c])

    def tags_copy(k):
        offset = AWAY if k == X else k - REACH
        return pltpu.make_async_copy(cluster_ref.at[block(offset * way)], tags.at[k], tags_sem.at[k])

    def remote(src, dst, send_sem, recv_sem, to):
        return pltpu.make_async_remote_copy(
            src_ref=src, dst_ref=dst, send_sem=send_sem, recv_sem=recv_sem, device_id=to, device_id_type=MESH
        )

    def own_copy(which, c):
        rows = chunk_rows(c)
        return remote(
            own.at[rows], near.at[which, rows], own_send.at[which, c], near_recv.at[which, c], device(1 - 2 * which)
        )

    def relay_copy(which, c):
        rows = chunk_rows(c)
        return remote(
            near.at[which, rows], far.at[which, rows], relay_send.at[c], far_recv.at[which, c], device(1 - 2 * which)
        )

    def relay2_copy(which, c):
        rows = chunk_rows(c)
        return remote(
            far.at[which, rows], third.at[which, rows], relay2_send.at[c], third_recv.at[which, c], device(1 - 2 * which)
        )

    def other_copy(c):
        rows = chunk_rows(c)
        return remote(far.at[chain, rows], other.at[rows], other_send.at[c], other_recv.at[c], other_core)

    each_chunk(lambda n: raw_copy(chunk(n)).start())
    for k in range(2 * REACH + 2):
        tags_copy(k).start()

    barrier = pltpu.get_barrier_semaphore()
    others = [k for k in range(-REACH, REACH + 1) if k != 0]
    met = [device(k) for k in others + [-AWAY, AWAY]] + [other_core]
    for to in met:
        pl.semaphore_signal(barrier, inc=1, device_id=to, device_id_type=MESH)

    def normalise(c):
        raw_copy(c).wait()

        def some(g, carry):
            rows = pl.ds(pl.multiple_of(c * CHUNK + g * 16, 16), 16)
            values = raw[rows].astype(jnp.float32)
            scale = lax.rsqrt(jnp.sum(values * values, axis=1, keepdims=True) + EPSILON)
            own[rows] = (values * scale).astype(jnp.bfloat16)
            return carry

        lax.fori_loop(0, CHUNK // 16, some, 0, unroll=2)

    def send_late(n):
        for h in range(2):
            own_copy(side, chunk(CHUNKS - 1 - 2 * n - h)).start()

    normalise(chunk(0))
    pl.semaphore_wait(barrier, len(met))
    own_copy(chain, chunk(0)).start()

    def send_step(n, carry):
        normalise(chunk(n))
        own_copy(chain, chunk(n)).start()
        return carry

    lax.fori_loop(1, CHUNKS, send_step, 0)

    @pl.when(seat == 7)
    def _():
        each_pair(send_late)

    row_sums[...] = jnp.zeros_like(row_sums)
    col_sums[...] = jnp.zeros_like(col_sums)
    for k in range(2 * REACH + 2):
        tags_copy(k).wait()

    def columns_of(c):
        for kind, at in DOWN.items():
            columns[at, chunk_rows(c)] = across(tags[kind, pl.ds(c, 1), :])

    each_chunk(columns_of)

    mine = tags[S]

    def edge_tag(k):
        numbers = tags[REACH + k * way]
        at = numbers[CHUNKS - 1 : CHUNKS, CHUNK - 1 : CHUNK] if k < 0 else numbers[0:1, 0:1]
        return jnp.broadcast_to(at, (CHUNKS, CHUNK))

    def total_of(values):
        return jnp.broadcast_to(jnp.sum(values, keepdims=True), (CHUNKS, CHUNK))

    def own_totals(column_values):
        totals = []
        for j in range(CHUNKS):

            def add(c, acc):
                same = columns[DOWN[S], chunk_rows(c)] == tags[S, j : j + 1, :]
                picked = jnp.where(same, column_values(c), 0.0)
                return acc + jnp.sum(picked.reshape(CHUNK // 8, 8, CHUNK), axis=0)

            acc = lax.fori_loop(0, CHUNKS, add, jnp.zeros((8, CHUNK), jnp.float32), unroll=True)
            totals.append(jnp.sum(acc, axis=0, keepdims=True))
        return jnp.concatenate(totals, axis=0)

    counts = own_totals(lambda c: 1.0)
    for k in others:
        edge = edge_tag(k)
        many = total_of(jnp.where(tags[REACH + k * way] == edge, 1.0, 0.0))
        counts = counts + jnp.where(mine == edge, many, 0.0)
        masks[others.index(k)] = jnp.where(mine == edge, 1.0, 0.0)
    row_counts[...] = counts
    first_tag = jnp.broadcast_to(mine[0:1, 0:1], (CHUNKS, CHUNK))
    last_tag = jnp.broadcast_to(mine[CHUNKS - 1 : CHUNKS, CHUNK - 1 : CHUNK], (CHUNKS, CHUNK))
    masks[len(others)] = jnp.where(mine == first_tag, 1.0, 0.0)
    masks[len(others) + 1] = jnp.where(mine == last_tag, 1.0, 0.0)

    refs = {S: own, C1: near.at[chain], C2: far.at[chain], C3: third.at[chain], P1: near.at[side], P2: far.at[side], X: other}

    def piece(arrived, c, resident, rows, size):
        scores = scores_of(refs[resident][rows], refs[arrived][pair_rows(c)])
        numbers = columns[DOWN[resident], rows]
        total = None
        for w in range(2):
            at = pl.ds(2 * c + w, 1)
            live = numbers == tags[arrived, at, :]
            if arrived == resident:
                place = lax.broadcasted_iota(jnp.int32, (size, CHUNK), 0) - (2 * c + w) * CHUNK
                live = live & (place != lax.broadcasted_iota(jnp.int32, (size, CHUNK), 1))
            cover = jnp.where(live, jnp.exp2(scores[:, w * CHUNK : (w + 1) * CHUNK] * GAIN - DROP), 0.0)
            total = cover if total is None else total + cover
            col_sums[ACROSS[arrived], at] += jnp.sum(cover.reshape(size // 8, 8, CHUNK), axis=0)[None]
        if arrived != resident:
            row_sums[DOWN[resident], rows] += total

    def strip(arrived, c, resident):
        piece(arrived, c, resident, pl.ds(0, ROWS), ROWS)

    def pieces(first, last, arrived, c_of, resident, r_of):
        def some(j, carry):
            piece(arrived, c_of(j), resident, pair_rows(r_of(j)), PAIR)
            return carry

        lax.fori_loop(first, last, some, 0)

    def sums_of(kind):
        total = None
        if kind in ACROSS:
            total = jnp.sum(col_sums[ACROSS[kind]], axis=1)
        if kind in DOWN:
            rows = [row_sums[DOWN[kind], c * CHUNK : (c + 1) * CHUNK] for c in range(CHUNKS)]
            total = total + jnp.concatenate([jnp.sum(jnp.transpose(r), axis=0, keepdims=True) for r in rows], axis=0)
        return total

    def part_copy(kind):
        offset = AWAY if kind == X else kind - REACH
        at = PART_OFFSETS.index(offset)
        at = jnp.where(leftward, at, len(PART_OFFSETS) - 1 - at)
        return at, remote(parts.at[at], parts_in.at[at], parts_send.at[at], parts_recv.at[at], device(offset * way))

    def send_part(kind):
        at, copy = part_copy(kind)
        parts[at] = sums_of(kind)
        copy.start()

    def part_comes(offset):
        at = lax.rem(d + (PERIOD - offset), PERIOD)
        left = (at >= 1) & (at <= 8)
        there = jnp.where(left, at - 1, lax.rem(PERIOD - at, PERIOD))
        rules = {1: there >= 0, 2: there <= 6, 3: there <= 3, -1: there <= 3, -2: there == 0, AWAY: (there >= 1) & (there <= 3)}
        comes = []
        if offset in rules:
            comes.append(left & rules[offset])
        if -offset in rules:
            comes.append(jnp.logical_not(left) & rules[-offset])
        return comes[0] if len(comes) == 1 else comes[0] | comes[1]

    def chunks_sent(c):
        own_copy(chain, c).wait_send()
        relay_copy(chain, c).wait_send()

        @pl.when(passes_own_back)
        def _():
            own_copy(side, c).wait_send()

        @pl.when(passes_c2)
        def _():
            relay2_copy(chain, c).wait_send()

        @pl.when(lends_c2)
        def _():
            other_copy(c).wait_send()

    each_pair(lambda c: strip(S, c, S))

    def near_step(n):
        for h in range(2):
            c = chunk(2 * n + h)
            own_copy(chain, c).wait_recv()

            @pl.when(seat != 0)
            def _():
                relay_copy(chain, c).start()

        @pl.when(d != 9)
        def _():
            strip(C1, pair(n), S)

    each_pair(near_step)

    @pl.when(seat >= 1)
    def _():
        send_part(C1)

    @pl.when(has_c2)
    def _():
        def far_step(n):
            for h in range(2):
                c = chunk(2 * n + h)
                relay_copy(chain, c).wait_recv()

                @pl.when(seat == 0)
                def _():
                    relay_copy(chain, c).start()

                @pl.when(passes_c2)
                def _():
                    relay2_copy(chain, c).start()

                @pl.when(lends_c2)
                def _():
                    other_copy(c).start()

            @pl.when((seat <= 2) & (n >= 2))
            def _():
                send_late(n - 2)

            strip(C2, pair(n), S)

        each_pair(far_step)

        @pl.when(seat >= 4)
        def _():
            send_part(C2)

    @pl.when(seat <= 2)
    def _():
        send_late(2)
        send_late(3)

    @pl.when(has_other)
    def _():
        def other_step(n):
            last = PAIRS - 1 - n
            for h in range(2):
                other_copy(chunk(2 * last + 1 - h)).wait_recv()
            pieces(last, PAIRS, X, lambda j: pair(last), C2, pair)

        each_pair(other_step)

    def side_step(n):
        last = PAIRS - 1 - n
        for h in range(2):
            own_copy(side, chunk(2 * last + 1 - h)).wait_recv()
        strip(P1, pair(last), C2)

    @pl.when(first_seat)
    def _():
        def first_step(n):
            side_step(n)
            strip(P1, pair(PAIRS - 1 - n), C1)

            @pl.when(d == 1)
            def _():
                strip(P1, pair(PAIRS - 1 - n), S)

        each_pair(first_step)

    @pl.when(has_c3)
    def _():
        def third_step(n):
            last = PAIRS - 1 - n
            for h in range(2):
                relay2_copy(chain, chunk(2 * n + h)).wait_recv()

            @pl.when(seat == 3)
            def _():
                strip(C3, pair(n), S)

            @pl.when(has_other & (d != 13))
            def _():
                strip(C3, pair(n), X)

            @pl.when(has_other)
            def _():
                side_step(n)

            pieces(jnp.maximum(n, last), PAIRS, C3, lambda j: pair(n), P1, pair)
            pieces(0, jnp.minimum(n, last + 1), C3, pair, P1, lambda j: pair(last))

            @pl.when(first_seat)
            def _():
                for h in range(2):
                    relay_copy(side, chunk(2 * last + 1 - h)).wait_recv()
                pieces(n, PAIRS, P2, lambda j: pair(last), C2, lambda j: pair(PAIRS - 1 - j))

                @pl.when(d == 1)
                def _():
                    strip(P2, pair(last), C1)

        each_pair(third_step)

    for kind, sends in ((C1, first_seat), (C2, has_c2 & (seat <= 3)), (C3, has_c3), (P1, has_p1), (P2, first_seat), (X, has_other)):

        @pl.when(sends)
        def _():
            send_part(kind)

    own_part[...] = sums_of(S)
    each_chunk(chunks_sent)

    for k, offset in enumerate(PART_OFFSETS):

        @pl.when(part_comes(offset))
        def _():
            remote(parts.at[k], parts_in.at[k], parts_send.at[k], parts_recv.at[k], device(offset)).wait_recv()
            own_part[...] += parts_in[k]

    total = own_part[...]
    cover = jnp.where(
        total < math.exp(-SHIFT),
        jnp.log1p(jnp.minimum(total, math.exp(-SHIFT)) * math.exp(SHIFT)),
        SHIFT + jnp.log(total + math.exp(-SHIFT)),
    )
    cover_ref[...] = cover

    for k in range(2):
        sums[k] = total_of(masks[len(others) + k] * cover)

    def sums_copy(k):
        at = others.index(k)
        return remote(sums.at[0 if k < 0 else 1], sums_in.at[at], sums_send.at[at], sums_recv.at[at], device(k))

    for k in others:
        sums_copy(k).start()
    for kind, sends in ((C1, seat >= 0), (C2, has_c2), (C3, has_c3), (P1, has_p1), (P2, first_seat), (X, has_other)):

        @pl.when(sends)
        def _():
            part_copy(kind)[1].wait_send()

    for c in range(CHUNKS):
        row_sums[0, c * CHUNK : (c + 1) * CHUNK] = across(cover[c : c + 1])
    cluster_sums = own_totals(lambda c: row_sums[0, chunk_rows(c)])
    for k in others:
        sums_copy(k).wait_recv()
        cluster_sums = cluster_sums + masks[others.index(-k)] * sums_in[others.index(k)]
    relative_ref[...] = cover - cluster_sums / row_counts[...]

    for k in others:
        sums_copy(k).wait_send()


def per_device(embeddings, cluster):
    rows, width = embeddings.shape
    vmem = pl.BlockSpec(memory_space=pltpu.VMEM)
    hbm = pl.BlockSpec(memory_space=pltpu.HBM)
    dma = pltpu.SemaphoreType.DMA
    small = (CHUNKS, CHUNK)
    cover, relative = pl.pallas_call(
        kernel,
        out_shape=[jax.ShapeDtypeStruct(small, jnp.float32)] * 2,
        in_specs=[hbm, hbm],
        out_specs=[vmem, vmem],
        scratch_shapes=[
            pltpu.VMEM((rows, width), jnp.bfloat16),
            pltpu.VMEM((rows, width), jnp.bfloat16),
            pltpu.VMEM((2, rows, width), jnp.bfloat16),
            pltpu.VMEM((2, rows, width), jnp.bfloat16),
            pltpu.VMEM((2, rows, width), jnp.bfloat16),
            pltpu.VMEM((rows, width), jnp.bfloat16),
            pltpu.VMEM((2 * REACH + 2, *small), jnp.int32),
            pltpu.VMEM((len(DOWN), rows, CHUNK), jnp.int32),
            pltpu.VMEM((len(DOWN), rows, CHUNK), jnp.float32),
            pltpu.VMEM((len(ACROSS), CHUNKS, 8, CHUNK), jnp.float32),
            pltpu.VMEM(small, jnp.float32),
            pltpu.VMEM((2 * REACH + 2, *small), jnp.float32),
            pltpu.VMEM(small, jnp.float32),
            pltpu.VMEM((len(PART_OFFSETS), *small), jnp.float32),
            pltpu.VMEM((len(PART_OFFSETS), *small), jnp.float32),
            pltpu.VMEM((2, *small), jnp.float32),
            pltpu.VMEM((2 * REACH, *small), jnp.float32),
            dma((CHUNKS,)),
            dma((2 * REACH + 2,)),
            dma((2, CHUNKS)),
            dma((2, CHUNKS)),
            dma((CHUNKS,)),
            dma((2, CHUNKS)),
            dma((CHUNKS,)),
            dma((2, CHUNKS)),
            dma((CHUNKS,)),
            dma((CHUNKS,)),
            dma((len(PART_OFFSETS),)),
            dma((len(PART_OFFSETS),)),
            dma((2 * REACH,)),
            dma((2 * REACH,)),
        ],
        compiler_params=pltpu.CompilerParams(
            collective_id=0, has_side_effects=True, vmem_limit_bytes=53 << 20
        ),
        name="cover",
    )(embeddings, cluster.reshape(-1, *small))
    return cover.reshape(rows), relative.reshape(rows)


def solution(mesh):
    placed = (P(("gx", "gy"), None), P())
    return jax.shard_map(
        per_device,
        mesh=mesh,
        in_specs=placed,
        out_specs=(P(("gx", "gy")), P(("gx", "gy"))),
        check_vma=False,
    )
```

```python
import math

import jax
import jax.numpy as jnp
from jax import lax
from jax.experimental import pallas as pl
from jax.experimental.pallas import tpu as pltpu
from jax.sharding import PartitionSpec as P

MESH = pl.DeviceIdType.MESH
INVERSE_TEMP = 100.0
EPSILON = 1e-06
SHIFT = 32.0
GAIN = INVERSE_TEMP * math.log2(math.e)
DROP = SHIFT * math.log2(math.e)

ROWS = 1024
CHUNK = 128
CHUNKS = ROWS // CHUNK
LEFT, RIGHT = 0, 1
REACH = 4
PERIOD = 16

S, C1, C2, C3, P1, P2, X = REACH, REACH + 1, REACH + 2, REACH + 3, REACH - 1, REACH - 2, 2 * REACH + 1
AWAY = 6
PART_OFFSETS = [-AWAY, -3, -2, -1, 1, 2, 3, AWAY]
PAIR = 2 * CHUNK
PAIRS = ROWS // PAIR
DOWN = {S: 0, C1: 1, C2: 2, P1: 3, X: 4}
ACROSS = {S: 0, C1: 1, C2: 2, C3: 3, P1: 4, P2: 5, X: 6}


def chunk_rows(c):
    return pl.ds(pl.multiple_of(c * CHUNK, CHUNK), CHUNK)


def pair_rows(c):
    return pl.ds(pl.multiple_of(c * PAIR, PAIR), PAIR)


def across(row):
    return jnp.transpose(jnp.broadcast_to(row, (CHUNK, CHUNK)))


def scores_of(left, right):
    return lax.dot_general(left, right, (((1,), (1,)), ((), ())), preferred_element_type=jnp.float32)


def log_of(total):
    return jnp.where(
        total < math.exp(-SHIFT),
        jnp.log1p(jnp.minimum(total, math.exp(-SHIFT)) * math.exp(SHIFT)),
        SHIFT + jnp.log(total + math.exp(-SHIFT)),
    )


def each_chunk(body):
    def step(c, carry):
        body(c)
        return carry

    lax.fori_loop(0, CHUNKS, step, 0)


def each_pair(body):
    def step(c, carry):
        body(c)
        return carry

    lax.fori_loop(0, PAIRS, step, 0)


def kernel(
    x_ref, cluster_ref, total_ref, mean_ref,
    raw, own, near, far, third, other, tags, columns, row_sums, col_sums, row_counts, masks, own_part, parts, parts_in, sums, sums_in,
    raw_sem, tags_sem, own_send, near_recv, relay_send, far_recv, relay2_send, third_recv, other_send, other_recv,
    parts_send, parts_recv, sums_send, sums_recv,
):
    gx, gy = lax.axis_index("gx"), lax.axis_index("gy")
    sizes = (lax.axis_size("gx"), lax.axis_size("gy"))
    devices = sizes[0] * sizes[1]
    me = gx * sizes[1] + gy

    d = lax.rem(me, PERIOD)
    leftward = (d >= 1) & (d <= 8)
    way = jnp.where(leftward, 1, -1)
    seat = jnp.where(leftward, d - 1, lax.rem(PERIOD - d, PERIOD))
    chain = jnp.where(leftward, RIGHT, LEFT)
    side = 1 - chain
    passes_own_back = (seat <= 2) | (seat == 7)
    has_c2 = seat <= 6
    has_c3 = seat <= 3
    has_p1 = seat <= 3
    first_seat = seat == 0
    passes_c2 = (seat >= 1) & (seat <= 4)
    lends_c2 = (seat >= 4) & (seat <= 6)
    has_other = (seat >= 1) & (seat <= 3)

    def block(offset):
        return lax.rem(me + (offset + devices), devices)

    def device(offset):
        place = block(offset)
        return (place // sizes[1], lax.rem(place, sizes[1]))

    def chunk(n):
        return jnp.where(leftward, n, CHUNKS - 1 - n)

    def pair(n):
        return jnp.where(leftward, n, PAIRS - 1 - n)

    other_core = (gx + 1 - 2 * lax.rem(gx, 2), gy)

    def raw_copy(c):
        return pltpu.make_async_copy(x_ref.at[chunk_rows(c)], raw.at[chunk_rows(c)], raw_sem.at[c])

    def tags_copy(k):
        offset = AWAY if k == X else k - REACH
        return pltpu.make_async_copy(cluster_ref.at[block(offset * way)], tags.at[k], tags_sem.at[k])

    def remote(src, dst, send_sem, recv_sem, to):
        return pltpu.make_async_remote_copy(
            src_ref=src, dst_ref=dst, send_sem=send_sem, recv_sem=recv_sem, device_id=to, device_id_type=MESH
        )

    def own_copy(which, c):
        rows = chunk_rows(c)
        return remote(
            own.at[rows], near.at[which, rows], own_send.at[which, c], near_recv.at[which, c], device(1 - 2 * which)
        )

    def relay_copy(which, c):
        rows = chunk_rows(c)
        return remote(
            near.at[which, rows], far.at[which, rows], relay_send.at[c], far_recv.at[which, c], device(1 - 2 * which)
        )

    def relay2_copy(which, c):
        rows = chunk_rows(c)
        return remote(
            far.at[which, rows], third.at[which, rows], relay2_send.at[c], third_recv.at[which, c], device(1 - 2 * which)
        )

    def other_copy(c):
        rows = chunk_rows(c)
        return remote(far.at[chain, rows], other.at[rows], other_send.at[c], other_recv.at[c], other_core)

    each_chunk(lambda n: raw_copy(chunk(n)).start())
    for k in range(2 * REACH + 2):
        tags_copy(k).start()

    barrier = pltpu.get_barrier_semaphore()
    others = [k for k in range(-REACH, REACH + 1) if k != 0]
    met = [device(k) for k in others + [-AWAY, AWAY]] + [other_core]
    for to in met:
        pl.semaphore_signal(barrier, inc=1, device_id=to, device_id_type=MESH)

    def normalise(c):
        raw_copy(c).wait()

        def some(g, carry):
            rows = pl.ds(pl.multiple_of(c * CHUNK + g * 16, 16), 16)
            values = raw[rows].astype(jnp.float32)
            scale = lax.rsqrt(jnp.sum(values * values, axis=1, keepdims=True) + EPSILON)
            own[rows] = (values * scale).astype(jnp.bfloat16)
            return carry

        lax.fori_loop(0, CHUNK // 16, some, 0, unroll=2)

    def send_late(n):
        for h in range(2):
            own_copy(side, chunk(CHUNKS - 1 - 2 * n - h)).start()

    normalise(chunk(0))
    pl.semaphore_wait(barrier, len(met))
    own_copy(chain, chunk(0)).start()

    def send_step(n, carry):
        normalise(chunk(n))
        own_copy(chain, chunk(n)).start()
        return carry

    lax.fori_loop(1, CHUNKS, send_step, 0)

    @pl.when(seat == 7)
    def _():
        each_pair(send_late)

    row_sums[...] = jnp.zeros_like(row_sums)
    col_sums[...] = jnp.zeros_like(col_sums)
    for k in range(2 * REACH + 2):
        tags_copy(k).wait()

    def columns_of(c):
        for kind, at in DOWN.items():
            columns[at, chunk_rows(c)] = across(tags[kind, pl.ds(c, 1), :])

    each_chunk(columns_of)

    mine = tags[S]

    def edge_tag(k):
        numbers = tags[REACH + k * way]
        at = numbers[CHUNKS - 1 : CHUNKS, CHUNK - 1 : CHUNK] if k < 0 else numbers[0:1, 0:1]
        return jnp.broadcast_to(at, (CHUNKS, CHUNK))

    def total_of(values):
        return jnp.broadcast_to(jnp.sum(values, keepdims=True), (CHUNKS, CHUNK))

    def own_totals(column_values):
        totals = []
        for j in range(CHUNKS):

            def add(c, acc):
                same = columns[DOWN[S], chunk_rows(c)] == tags[S, j : j + 1, :]
                picked = jnp.where(same, column_values(c), 0.0)
                return acc + jnp.sum(picked.reshape(CHUNK // 8, 8, CHUNK), axis=0)

            acc = lax.fori_loop(0, CHUNKS, add, jnp.zeros((8, CHUNK), jnp.float32), unroll=True)
            totals.append(jnp.sum(acc, axis=0, keepdims=True))
        return jnp.concatenate(totals, axis=0)

    counts = own_totals(lambda c: 1.0)
    for k in others:
        edge = edge_tag(k)
        many = total_of(jnp.where(tags[REACH + k * way] == edge, 1.0, 0.0))
        counts = counts + jnp.where(mine == edge, many, 0.0)
        masks[others.index(k)] = jnp.where(mine == edge, 1.0, 0.0)
    row_counts[...] = counts
    first_tag = jnp.broadcast_to(mine[0:1, 0:1], (CHUNKS, CHUNK))
    last_tag = jnp.broadcast_to(mine[CHUNKS - 1 : CHUNKS, CHUNK - 1 : CHUNK], (CHUNKS, CHUNK))
    masks[len(others)] = jnp.where(mine == first_tag, 1.0, 0.0)
    masks[len(others) + 1] = jnp.where(mine == last_tag, 1.0, 0.0)

    refs = {S: own, C1: near.at[chain], C2: far.at[chain], C3: third.at[chain], P1: near.at[side], P2: far.at[side], X: other}

    def piece(arrived, c, resident, rows, size):
        scores = scores_of(refs[resident][rows], refs[arrived][pair_rows(c)])
        numbers = columns[DOWN[resident], rows]
        total = None
        for w in range(2):
            at = pl.ds(2 * c + w, 1)
            live = numbers == tags[arrived, at, :]
            if arrived == resident:
                place = lax.broadcasted_iota(jnp.int32, (size, CHUNK), 0) - (2 * c + w) * CHUNK
                live = live & (place != lax.broadcasted_iota(jnp.int32, (size, CHUNK), 1))
            cover = jnp.where(live, jnp.exp2(scores[:, w * CHUNK : (w + 1) * CHUNK] * GAIN - DROP), 0.0)
            total = cover if total is None else total + cover
            col_sums[ACROSS[arrived], at] += jnp.sum(cover.reshape(size // 8, 8, CHUNK), axis=0)[None]
        if arrived != resident:
            row_sums[DOWN[resident], rows] += total

    def strip(arrived, c, resident):
        piece(arrived, c, resident, pl.ds(0, ROWS), ROWS)

    def pieces(first, last, arrived, c_of, resident, r_of):
        def some(j, carry):
            piece(arrived, c_of(j), resident, pair_rows(r_of(j)), PAIR)
            return carry

        lax.fori_loop(first, last, some, 0)

    def sums_of(kind):
        total = None
        if kind in ACROSS:
            total = jnp.sum(col_sums[ACROSS[kind]], axis=1)
        if kind in DOWN:
            rows = [row_sums[DOWN[kind], c * CHUNK : (c + 1) * CHUNK] for c in range(CHUNKS)]
            total = total + jnp.concatenate([jnp.sum(jnp.transpose(r), axis=0, keepdims=True) for r in rows], axis=0)
        return total

    def part_copy(kind):
        offset = AWAY if kind == X else kind - REACH
        at = PART_OFFSETS.index(offset)
        at = jnp.where(leftward, at, len(PART_OFFSETS) - 1 - at)
        return at, remote(parts.at[at], parts_in.at[at], parts_send.at[at], parts_recv.at[at], device(offset * way))

    def send_part(kind):
        at, copy = part_copy(kind)
        parts[at] = sums_of(kind)
        copy.start()

    def part_comes(offset):
        at = lax.rem(d + (PERIOD - offset), PERIOD)
        left = (at >= 1) & (at <= 8)
        there = jnp.where(left, at - 1, lax.rem(PERIOD - at, PERIOD))
        rules = {1: there >= 0, 2: there <= 6, 3: there <= 3, -1: there <= 3, -2: there == 0, AWAY: (there >= 1) & (there <= 3)}
        comes = []
        if offset in rules:
            comes.append(left & rules[offset])
        if -offset in rules:
            comes.append(jnp.logical_not(left) & rules[-offset])
        return comes[0] if len(comes) == 1 else comes[0] | comes[1]

    def chunks_sent(c):
        own_copy(chain, c).wait_send()
        relay_copy(chain, c).wait_send()

        @pl.when(passes_own_back)
        def _():
            own_copy(side, c).wait_send()

        @pl.when(passes_c2)
        def _():
            relay2_copy(chain, c).wait_send()

        @pl.when(lends_c2)
        def _():
            other_copy(c).wait_send()

    each_pair(lambda c: strip(S, c, S))

    def near_step(n):
        for h in range(2):
            c = chunk(2 * n + h)
            own_copy(chain, c).wait_recv()

            @pl.when(seat != 0)
            def _():
                relay_copy(chain, c).start()

        @pl.when(d != 9)
        def _():
            strip(C1, pair(n), S)

    each_pair(near_step)

    @pl.when(seat >= 1)
    def _():
        send_part(C1)

    @pl.when(has_c2)
    def _():
        def far_step(n):
            for h in range(2):
                c = chunk(2 * n + h)
                relay_copy(chain, c).wait_recv()

                @pl.when(seat == 0)
                def _():
                    relay_copy(chain, c).start()

                @pl.when(passes_c2)
                def _():
                    relay2_copy(chain, c).start()

                @pl.when(lends_c2)
                def _():
                    other_copy(c).start()

            @pl.when((seat <= 2) & (n >= 2))
            def _():
                send_late(n - 2)

            strip(C2, pair(n), S)

        each_pair(far_step)

        @pl.when(seat >= 4)
        def _():
            send_part(C2)

    @pl.when(seat <= 2)
    def _():
        send_late(2)
        send_late(3)

    @pl.when(has_other)
    def _():
        def other_step(n):
            last = PAIRS - 1 - n
            for h in range(2):
                other_copy(chunk(2 * last + 1 - h)).wait_recv()
            pieces(last, PAIRS, X, lambda j: pair(last), C2, pair)

        each_pair(other_step)

    def side_step(n):
        last = PAIRS - 1 - n
        for h in range(2):
            own_copy(side, chunk(2 * last + 1 - h)).wait_recv()
        strip(P1, pair(last), C2)

    @pl.when(first_seat)
    def _():
        def first_step(n):
            side_step(n)
            strip(P1, pair(PAIRS - 1 - n), C1)

            @pl.when(d == 1)
            def _():
                strip(P1, pair(PAIRS - 1 - n), S)

        each_pair(first_step)

    @pl.when(has_c3)
    def _():
        def third_step(n):
            last = PAIRS - 1 - n
            for h in range(2):
                relay2_copy(chain, chunk(2 * n + h)).wait_recv()

            @pl.when(seat == 3)
            def _():
                strip(C3, pair(n), S)

            @pl.when(has_other & (d != 13))
            def _():
                strip(C3, pair(n), X)

            @pl.when(has_other)
            def _():
                side_step(n)

            pieces(jnp.maximum(n, last), PAIRS, C3, lambda j: pair(n), P1, pair)
            pieces(0, jnp.minimum(n, last + 1), C3, pair, P1, lambda j: pair(last))

            @pl.when(first_seat)
            def _():
                for h in range(2):
                    relay_copy(side, chunk(2 * last + 1 - h)).wait_recv()
                pieces(n, PAIRS, P2, lambda j: pair(last), C2, lambda j: pair(PAIRS - 1 - j))

                @pl.when(d == 1)
                def _():
                    strip(P2, pair(last), C1)

        each_pair(third_step)

    for kind, sends in ((X, has_other), (C3, has_c3), (P2, first_seat), (C2, has_c2 & (seat <= 3)), (P1, has_p1), (C1, first_seat)):

        @pl.when(sends)
        def _():
            send_part(kind)

    own_part[...] = sums_of(S)
    each_chunk(chunks_sent)

    for k, offset in enumerate(PART_OFFSETS):

        @pl.when(part_comes(offset))
        def _():
            remote(parts.at[k], parts_in.at[k], parts_send.at[k], parts_recv.at[k], device(offset)).wait_recv()
            own_part[...] += parts_in[k]

    total = own_part[...]
    cover = log_of(total)
    total_ref[...] = total

    for k in range(2):
        sums[k] = total_of(masks[len(others) + k] * cover)

    def sums_copy(k):
        at = others.index(k)
        return remote(sums.at[0 if k < 0 else 1], sums_in.at[at], sums_send.at[at], sums_recv.at[at], device(k))

    for k in sorted(others, key=abs, reverse=True):
        sums_copy(k).start()
    for kind, sends in ((C1, seat >= 0), (C2, has_c2), (C3, has_c3), (P1, has_p1), (P2, first_seat), (X, has_other)):

        @pl.when(sends)
        def _():
            part_copy(kind)[1].wait_send()

    for c in range(CHUNKS):
        row_sums[0, c * CHUNK : (c + 1) * CHUNK] = across(cover[c : c + 1])
    cluster_sums = own_totals(lambda c: row_sums[0, chunk_rows(c)])
    for k in others:
        sums_copy(k).wait_recv()
        cluster_sums = cluster_sums + masks[others.index(-k)] * sums_in[others.index(k)]
    mean_ref[...] = cluster_sums / row_counts[...]

    for k in others:
        sums_copy(k).wait_send()


def per_device(embeddings, cluster):
    rows, width = embeddings.shape
    vmem = pl.BlockSpec(memory_space=pltpu.VMEM)
    hbm = pl.BlockSpec(memory_space=pltpu.HBM)
    dma = pltpu.SemaphoreType.DMA
    small = (CHUNKS, CHUNK)
    total, mean = pl.pallas_call(
        kernel,
        out_shape=[jax.ShapeDtypeStruct(small, jnp.float32)] * 2,
        in_specs=[hbm, hbm],
        out_specs=[vmem, vmem],
        scratch_shapes=[
            pltpu.VMEM((rows, width), jnp.bfloat16),
            pltpu.VMEM((rows, width), jnp.bfloat16),
            pltpu.VMEM((2, rows, width), jnp.bfloat16),
            pltpu.VMEM((2, rows, width), jnp.bfloat16),
            pltpu.VMEM((2, rows, width), jnp.bfloat16),
            pltpu.VMEM((rows, width), jnp.bfloat16),
            pltpu.VMEM((2 * REACH + 2, *small), jnp.int32),
            pltpu.VMEM((len(DOWN), rows, CHUNK), jnp.int32),
            pltpu.VMEM((len(DOWN), rows, CHUNK), jnp.float32),
            pltpu.VMEM((len(ACROSS), CHUNKS, 8, CHUNK), jnp.float32),
            pltpu.VMEM(small, jnp.float32),
            pltpu.VMEM((2 * REACH + 2, *small), jnp.float32),
            pltpu.VMEM(small, jnp.float32),
            pltpu.VMEM((len(PART_OFFSETS), *small), jnp.float32),
            pltpu.VMEM((len(PART_OFFSETS), *small), jnp.float32),
            pltpu.VMEM((2, *small), jnp.float32),
            pltpu.VMEM((2 * REACH, *small), jnp.float32),
            dma((CHUNKS,)),
            dma((2 * REACH + 2,)),
            dma((2, CHUNKS)),
            dma((2, CHUNKS)),
            dma((CHUNKS,)),
            dma((2, CHUNKS)),
            dma((CHUNKS,)),
            dma((2, CHUNKS)),
            dma((CHUNKS,)),
            dma((CHUNKS,)),
            dma((len(PART_OFFSETS),)),
            dma((len(PART_OFFSETS),)),
            dma((2 * REACH,)),
            dma((2 * REACH,)),
        ],
        compiler_params=pltpu.CompilerParams(
            collective_id=0, has_side_effects=True, vmem_limit_bytes=53 << 20
        ),
        name="cover",
    )(embeddings, cluster.reshape(-1, *small))
    cover = log_of(total.reshape(rows))
    return cover, cover - mean.reshape(rows)


def solution(mesh):
    placed = (P(("gx", "gy"), None), P())
    return jax.shard_map(
        per_device,
        mesh=mesh,
        in_specs=placed,
        out_specs=(P(("gx", "gy")), P(("gx", "gy"))),
        check_vma=False,
    )
```

```python
import math

import jax
import jax.numpy as jnp
from jax import lax
from jax.experimental import pallas as pl
from jax.experimental.pallas import tpu as pltpu
from jax.sharding import PartitionSpec as P

MESH = pl.DeviceIdType.MESH
INVERSE_TEMP = 100.0
EPSILON = 1e-06
SHIFT = 32.0
GAIN = INVERSE_TEMP * math.log2(math.e)
DROP = SHIFT * math.log2(math.e)

ROWS = 1024
CHUNK = 128
CHUNKS = ROWS // CHUNK
LEFT, RIGHT = 0, 1
REACH = 4
PERIOD = 16

S, C1, C2, C3, P1, P2, X = REACH, REACH + 1, REACH + 2, REACH + 3, REACH - 1, REACH - 2, 2 * REACH + 1
AWAY = 6
PART_OFFSETS = [-AWAY, -3, -2, -1, 1, 2, 3, AWAY]
PAIR = 2 * CHUNK
PAIRS = ROWS // PAIR
DOWN = {S: 0, C1: 1, C2: 2, P1: 3, X: 4}
ACROSS = {S: 0, C1: 1, C2: 2, C3: 3, P1: 4, P2: 5, X: 6}


def chunk_rows(c):
    return pl.ds(pl.multiple_of(c * CHUNK, CHUNK), CHUNK)


def pair_rows(c):
    return pl.ds(pl.multiple_of(c * PAIR, PAIR), PAIR)


def across(row):
    return jnp.transpose(jnp.broadcast_to(row, (CHUNK, CHUNK)))


def scores_of(left, right):
    return lax.dot_general(left, right, (((1,), (1,)), ((), ())), preferred_element_type=jnp.float32)


def log_of(total):
    return jnp.where(
        total < math.exp(-SHIFT),
        jnp.log1p(jnp.minimum(total, math.exp(-SHIFT)) * math.exp(SHIFT)),
        SHIFT + jnp.log(total + math.exp(-SHIFT)),
    )


def each_chunk(body):
    def step(c, carry):
        body(c)
        return carry

    lax.fori_loop(0, CHUNKS, step, 0)


def each_pair(body):
    def step(c, carry):
        body(c)
        return carry

    lax.fori_loop(0, PAIRS, step, 0)


def kernel(
    x_ref, cluster_ref, total_ref, mean_ref,
    raw, own, near, far, third, other, tags, columns, row_sums, col_sums, row_counts, masks, own_part, parts, parts_in, sums, sums_in,
    raw_sem, tags_sem, own_send, near_recv, relay_send, far_recv, relay2_send, third_recv, other_send, other_recv,
    parts_send, parts_recv, sums_send, sums_recv,
):
    gx, gy = lax.axis_index("gx"), lax.axis_index("gy")
    sizes = (lax.axis_size("gx"), lax.axis_size("gy"))
    devices = sizes[0] * sizes[1]
    me = gx * sizes[1] + gy

    d = lax.rem(me, PERIOD)
    leftward = (d >= 1) & (d <= 8)
    way = jnp.where(leftward, 1, -1)
    seat = jnp.where(leftward, d - 1, lax.rem(PERIOD - d, PERIOD))
    chain = jnp.where(leftward, RIGHT, LEFT)
    side = 1 - chain
    passes_own_back = (seat <= 2) | (seat == 7)
    has_c2 = seat <= 6
    has_c3 = seat <= 3
    has_p1 = seat <= 3
    first_seat = seat == 0
    passes_c2 = (seat >= 1) & (seat <= 4)
    lends_c2 = (seat >= 4) & (seat <= 6)
    has_other = (seat >= 1) & (seat <= 3)

    def block(offset):
        return lax.rem(me + (offset + devices), devices)

    def device(offset):
        place = block(offset)
        return (place // sizes[1], lax.rem(place, sizes[1]))

    def chunk(n):
        return jnp.where(leftward, n, CHUNKS - 1 - n)

    def pair(n):
        return jnp.where(leftward, n, PAIRS - 1 - n)

    other_core = (gx + 1 - 2 * lax.rem(gx, 2), gy)

    def raw_copy(c):
        return pltpu.make_async_copy(x_ref.at[chunk_rows(c)], raw.at[chunk_rows(c)], raw_sem.at[c])

    def tags_copy(k):
        offset = AWAY if k == X else k - REACH
        return pltpu.make_async_copy(cluster_ref.at[block(offset * way)], tags.at[k], tags_sem.at[k])

    def remote(src, dst, send_sem, recv_sem, to):
        return pltpu.make_async_remote_copy(
            src_ref=src, dst_ref=dst, send_sem=send_sem, recv_sem=recv_sem, device_id=to, device_id_type=MESH
        )

    def own_copy(which, c):
        rows = chunk_rows(c)
        return remote(
            own.at[rows], near.at[which, rows], own_send.at[which, c], near_recv.at[which, c], device(1 - 2 * which)
        )

    def relay_copy(which, c):
        rows = chunk_rows(c)
        return remote(
            near.at[which, rows], far.at[which, rows], relay_send.at[c], far_recv.at[which, c], device(1 - 2 * which)
        )

    def relay2_copy(which, c):
        rows = chunk_rows(c)
        return remote(
            far.at[which, rows], third.at[which, rows], relay2_send.at[c], third_recv.at[which, c], device(1 - 2 * which)
        )

    def other_copy(c):
        rows = chunk_rows(c)
        return remote(far.at[chain, rows], other.at[rows], other_send.at[c], other_recv.at[c], other_core)

    raw_copy(chunk(0)).start()
    barrier = pltpu.get_barrier_semaphore()
    others = [k for k in range(-REACH, REACH + 1) if k != 0]
    met = [device(k) for k in others + [-AWAY, AWAY]] + [other_core]
    for to in met:
        pl.semaphore_signal(barrier, inc=1, device_id=to, device_id_type=MESH)
    for n in range(1, CHUNKS):
        raw_copy(chunk(n)).start()
    for k in range(2 * REACH + 2):
        tags_copy(k).start()

    def normalise(c):
        raw_copy(c).wait()

        def some(g, carry):
            rows = pl.ds(pl.multiple_of(c * CHUNK + g * 16, 16), 16)
            values = raw[rows].astype(jnp.float32)
            scale = lax.rsqrt(jnp.sum(values * values, axis=1, keepdims=True) + EPSILON)
            own[rows] = (values * scale).astype(jnp.bfloat16)
            return carry

        lax.fori_loop(0, CHUNK // 16, some, 0, unroll=2)

    def send_late(n):
        for h in range(2):
            own_copy(side, chunk(CHUNKS - 1 - 2 * n - h)).start()

    normalise(chunk(0))
    pl.semaphore_wait(barrier, len(met))
    own_copy(chain, chunk(0)).start()

    def send_step(n, carry):
        normalise(chunk(n))
        own_copy(chain, chunk(n)).start()
        return carry

    lax.fori_loop(1, CHUNKS, send_step, 0)

    @pl.when(seat == 7)
    def _():
        each_pair(send_late)

    row_sums[...] = jnp.zeros_like(row_sums)
    col_sums[...] = jnp.zeros_like(col_sums)
    for k in range(2 * REACH + 2):
        tags_copy(k).wait()

    def columns_of(c):
        for kind, at in DOWN.items():
            columns[at, chunk_rows(c)] = across(tags[kind, pl.ds(c, 1), :])

    each_chunk(columns_of)

    mine = tags[S]

    def edge_tag(k):
        numbers = tags[REACH + k * way]
        at = numbers[CHUNKS - 1 : CHUNKS, CHUNK - 1 : CHUNK] if k < 0 else numbers[0:1, 0:1]
        return jnp.broadcast_to(at, (CHUNKS, CHUNK))

    def total_of(values):
        return jnp.broadcast_to(jnp.sum(values, keepdims=True), (CHUNKS, CHUNK))

    def own_totals(column_values):
        totals = []
        for j in range(CHUNKS):

            def add(c, acc):
                same = columns[DOWN[S], chunk_rows(c)] == tags[S, j : j + 1, :]
                picked = jnp.where(same, column_values(c), 0.0)
                return acc + jnp.sum(picked.reshape(CHUNK // 8, 8, CHUNK), axis=0)

            acc = lax.fori_loop(0, CHUNKS, add, jnp.zeros((8, CHUNK), jnp.float32), unroll=True)
            totals.append(jnp.sum(acc, axis=0, keepdims=True))
        return jnp.concatenate(totals, axis=0)

    counts = own_totals(lambda c: 1.0)
    for k in others:
        edge = edge_tag(k)
        many = total_of(jnp.where(tags[REACH + k * way] == edge, 1.0, 0.0))
        counts = counts + jnp.where(mine == edge, many, 0.0)
        masks[others.index(k)] = jnp.where(mine == edge, 1.0, 0.0)
    row_counts[...] = counts
    first_tag = jnp.broadcast_to(mine[0:1, 0:1], (CHUNKS, CHUNK))
    last_tag = jnp.broadcast_to(mine[CHUNKS - 1 : CHUNKS, CHUNK - 1 : CHUNK], (CHUNKS, CHUNK))
    masks[len(others)] = jnp.where(mine == first_tag, 1.0, 0.0)
    masks[len(others) + 1] = jnp.where(mine == last_tag, 1.0, 0.0)

    refs = {S: own, C1: near.at[chain], C2: far.at[chain], C3: third.at[chain], P1: near.at[side], P2: far.at[side], X: other}

    def piece(arrived, c, resident, rows, size):
        scores = scores_of(refs[resident][rows], refs[arrived][pair_rows(c)])
        numbers = columns[DOWN[resident], rows]
        total = None
        for w in range(2):
            at = pl.ds(2 * c + w, 1)
            live = numbers == tags[arrived, at, :]
            if arrived == resident:
                place = lax.broadcasted_iota(jnp.int32, (size, CHUNK), 0) - (2 * c + w) * CHUNK
                live = live & (place != lax.broadcasted_iota(jnp.int32, (size, CHUNK), 1))
            cover = jnp.where(live, jnp.exp2(scores[:, w * CHUNK : (w + 1) * CHUNK] * GAIN - DROP), 0.0)
            total = cover if total is None else total + cover
            col_sums[ACROSS[arrived], at] += jnp.sum(cover.reshape(size // 8, 8, CHUNK), axis=0)[None]
        if arrived != resident:
            row_sums[DOWN[resident], rows] += total

    def strip(arrived, c, resident):
        piece(arrived, c, resident, pl.ds(0, ROWS), ROWS)

    def pieces(first, last, arrived, c_of, resident, r_of):
        def some(j, carry):
            piece(arrived, c_of(j), resident, pair_rows(r_of(j)), PAIR)
            return carry

        lax.fori_loop(first, last, some, 0)

    def sums_of(kind):
        total = None
        if kind in ACROSS:
            total = jnp.sum(col_sums[ACROSS[kind]], axis=1)
        if kind in DOWN:
            rows = [row_sums[DOWN[kind], c * CHUNK : (c + 1) * CHUNK] for c in range(CHUNKS)]
            total = total + jnp.concatenate([jnp.sum(jnp.transpose(r), axis=0, keepdims=True) for r in rows], axis=0)
        return total

    def part_copy(kind):
        offset = AWAY if kind == X else kind - REACH
        at = PART_OFFSETS.index(offset)
        at = jnp.where(leftward, at, len(PART_OFFSETS) - 1 - at)
        return at, remote(parts.at[at], parts_in.at[at], parts_send.at[at], parts_recv.at[at], device(offset * way))

    def send_part(kind):
        at, copy = part_copy(kind)
        parts[at] = sums_of(kind)
        copy.start()

    def part_comes(offset):
        at = lax.rem(d + (PERIOD - offset), PERIOD)
        left = (at >= 1) & (at <= 8)
        there = jnp.where(left, at - 1, lax.rem(PERIOD - at, PERIOD))
        rules = {1: there >= 0, 2: there <= 6, 3: there <= 3, -1: there <= 3, -2: there == 0, AWAY: (there >= 1) & (there <= 3)}
        comes = []
        if offset in rules:
            comes.append(left & rules[offset])
        if -offset in rules:
            comes.append(jnp.logical_not(left) & rules[-offset])
        return comes[0] if len(comes) == 1 else comes[0] | comes[1]

    def chunks_sent(c):
        own_copy(chain, c).wait_send()
        relay_copy(chain, c).wait_send()

        @pl.when(passes_own_back)
        def _():
            own_copy(side, c).wait_send()

        @pl.when(passes_c2)
        def _():
            relay2_copy(chain, c).wait_send()

        @pl.when(lends_c2)
        def _():
            other_copy(c).wait_send()

    each_pair(lambda c: strip(S, c, S))

    def near_step(n):
        for h in range(2):
            c = chunk(2 * n + h)
            own_copy(chain, c).wait_recv()

            @pl.when(seat != 0)
            def _():
                relay_copy(chain, c).start()

        @pl.when(d != 9)
        def _():
            strip(C1, pair(n), S)

    each_pair(near_step)

    @pl.when(seat >= 1)
    def _():
        send_part(C1)

    @pl.when(has_c2)
    def _():
        def far_step(n):
            for h in range(2):
                c = chunk(2 * n + h)
                relay_copy(chain, c).wait_recv()

                @pl.when(seat == 0)
                def _():
                    relay_copy(chain, c).start()

                @pl.when(passes_c2)
                def _():
                    relay2_copy(chain, c).start()

                @pl.when(lends_c2)
                def _():
                    other_copy(c).start()

            @pl.when((seat <= 2) & (n >= 2))
            def _():
                send_late(n - 2)

            strip(C2, pair(n), S)

        each_pair(far_step)

        @pl.when(seat >= 4)
        def _():
            send_part(C2)

    @pl.when(seat <= 2)
    def _():
        send_late(2)
        send_late(3)

    @pl.when(has_other)
    def _():
        def other_step(n):
            last = PAIRS - 1 - n
            for h in range(2):
                other_copy(chunk(2 * last + 1 - h)).wait_recv()
            pieces(last, PAIRS, X, lambda j: pair(last), C2, pair)

        each_pair(other_step)

    def side_step(n):
        last = PAIRS - 1 - n
        for h in range(2):
            own_copy(side, chunk(2 * last + 1 - h)).wait_recv()
        strip(P1, pair(last), C2)

    @pl.when(first_seat)
    def _():
        def first_step(n):
            side_step(n)
            strip(P1, pair(PAIRS - 1 - n), C1)

            @pl.when(d == 1)
            def _():
                strip(P1, pair(PAIRS - 1 - n), S)

        each_pair(first_step)

    @pl.when(has_c3)
    def _():
        def third_step(n):
            last = PAIRS - 1 - n
            for h in range(2):
                relay2_copy(chain, chunk(2 * n + h)).wait_recv()

            @pl.when(seat == 3)
            def _():
                strip(C3, pair(n), S)

            @pl.when(has_other & (d != 13))
            def _():
                strip(C3, pair(n), X)

            @pl.when(has_other & (n == PAIRS - 1))
            def _():
                send_part(X)

            @pl.when(has_other)
            def _():
                side_step(n)

            pieces(jnp.maximum(n, last), PAIRS, C3, lambda j: pair(n), P1, pair)
            pieces(0, jnp.minimum(n, last + 1), C3, pair, P1, lambda j: pair(last))

            @pl.when(first_seat & (n == PAIRS - 1))
            def _():
                send_part(C3)
                send_part(P1)

            @pl.when(first_seat)
            def _():
                for h in range(2):
                    relay_copy(side, chunk(2 * last + 1 - h)).wait_recv()
                pieces(n, PAIRS, P2, lambda j: pair(last), C2, lambda j: pair(PAIRS - 1 - j))

                @pl.when(d == 1)
                def _():
                    strip(P2, pair(last), C1)

        each_pair(third_step)

    for kind, sends in ((C3, has_other), (P2, first_seat), (C2, has_c2 & (seat <= 3)), (P1, has_other), (C1, first_seat)):

        @pl.when(sends)
        def _():
            send_part(kind)

    own_part[...] = sums_of(S)
    each_chunk(chunks_sent)

    for k, offset in enumerate(PART_OFFSETS):

        @pl.when(part_comes(offset))
        def _():
            remote(parts.at[k], parts_in.at[k], parts_send.at[k], parts_recv.at[k], device(offset)).wait_recv()
            own_part[...] += parts_in[k]

    total = own_part[...]
    cover = log_of(total)
    total_ref[...] = total

    for k in range(2):
        sums[k] = total_of(masks[len(others) + k] * cover)

    def sums_copy(k):
        at = others.index(k)
        return remote(sums.at[0 if k < 0 else 1, 0:1], sums_in.at[at, 0:1], sums_send.at[at], sums_recv.at[at], device(k))

    for k in sorted(others, key=abs, reverse=True):
        sums_copy(k).start()
    for kind, sends in ((C1, seat >= 0), (C2, has_c2), (C3, has_c3), (P1, has_p1), (P2, first_seat), (X, has_other)):

        @pl.when(sends)
        def _():
            part_copy(kind)[1].wait_send()

    for c in range(CHUNKS):
        row_sums[0, c * CHUNK : (c + 1) * CHUNK] = across(cover[c : c + 1])
    cluster_sums = own_totals(lambda c: row_sums[0, chunk_rows(c)])
    for k in others:
        sums_copy(k).wait_recv()
        cluster_sums = cluster_sums + masks[others.index(-k)] * sums_in[others.index(k), 0:1]
    mean_ref[...] = cluster_sums / row_counts[...]

    for k in others:
        sums_copy(k).wait_send()


def per_device(embeddings, cluster):
    rows, width = embeddings.shape
    vmem = pl.BlockSpec(memory_space=pltpu.VMEM)
    hbm = pl.BlockSpec(memory_space=pltpu.HBM)
    dma = pltpu.SemaphoreType.DMA
    small = (CHUNKS, CHUNK)
    total, mean = pl.pallas_call(
        kernel,
        out_shape=[jax.ShapeDtypeStruct(small, jnp.float32)] * 2,
        in_specs=[hbm, hbm],
        out_specs=[vmem, vmem],
        scratch_shapes=[
            pltpu.VMEM((rows, width), jnp.bfloat16),
            pltpu.VMEM((rows, width), jnp.bfloat16),
            pltpu.VMEM((2, rows, width), jnp.bfloat16),
            pltpu.VMEM((2, rows, width), jnp.bfloat16),
            pltpu.VMEM((2, rows, width), jnp.bfloat16),
            pltpu.VMEM((rows, width), jnp.bfloat16),
            pltpu.VMEM((2 * REACH + 2, *small), jnp.int32),
            pltpu.VMEM((len(DOWN), rows, CHUNK), jnp.int32),
            pltpu.VMEM((len(DOWN), rows, CHUNK), jnp.float32),
            pltpu.VMEM((len(ACROSS), CHUNKS, 8, CHUNK), jnp.float32),
            pltpu.VMEM(small, jnp.float32),
            pltpu.VMEM((2 * REACH + 2, *small), jnp.float32),
            pltpu.VMEM(small, jnp.float32),
            pltpu.VMEM((len(PART_OFFSETS), *small), jnp.float32),
            pltpu.VMEM((len(PART_OFFSETS), *small), jnp.float32),
            pltpu.VMEM((2, *small), jnp.float32),
            pltpu.VMEM((2 * REACH, *small), jnp.float32),
            dma((CHUNKS,)),
            dma((2 * REACH + 2,)),
            dma((2, CHUNKS)),
            dma((2, CHUNKS)),
            dma((CHUNKS,)),
            dma((2, CHUNKS)),
            dma((CHUNKS,)),
            dma((2, CHUNKS)),
            dma((CHUNKS,)),
            dma((CHUNKS,)),
            dma((len(PART_OFFSETS),)),
            dma((len(PART_OFFSETS),)),
            dma((2 * REACH,)),
            dma((2 * REACH,)),
        ],
        compiler_params=pltpu.CompilerParams(
            collective_id=0, has_side_effects=True, vmem_limit_bytes=53 << 20
        ),
        name="cover",
    )(embeddings, cluster.reshape(-1, *small))
    cover = log_of(total.reshape(rows))
    return cover, cover - mean.reshape(rows)


def solution(mesh):
    placed = (P(("gx", "gy"), None), P())
    return jax.shard_map(
        per_device,
        mesh=mesh,
        in_specs=placed,
        out_specs=(P(("gx", "gy")), P(("gx", "gy"))),
        check_vma=False,
    )
```

```python
import math

import jax
import jax.numpy as jnp
from jax import lax
from jax.experimental import pallas as pl
from jax.experimental.pallas import tpu as pltpu
from jax.sharding import PartitionSpec as P

MESH = pl.DeviceIdType.MESH
INVERSE_TEMP = 100.0
EPSILON = 1e-06
SHIFT = 32.0
GAIN = INVERSE_TEMP * math.log2(math.e)
DROP = SHIFT * math.log2(math.e)

ROWS = 1024
CHUNK = 128
CHUNKS = ROWS // CHUNK
LEFT, RIGHT = 0, 1
REACH = 4
PERIOD = 16

S, C1, C2, C3, P1, P2, X = REACH, REACH + 1, REACH + 2, REACH + 3, REACH - 1, REACH - 2, 2 * REACH + 1
AWAY = 6
PART_OFFSETS = [-AWAY, -3, -2, -1, 1, 2, 3, AWAY]
PAIR = 2 * CHUNK
PAIRS = ROWS // PAIR
DOWN = {S: 0, C1: 1, C2: 2, P1: 3, X: 4}
ACROSS = {S: 0, C1: 1, C2: 2, C3: 3, P1: 4, P2: 5, X: 6}


def chunk_rows(c):
    return pl.ds(pl.multiple_of(c * CHUNK, CHUNK), CHUNK)


def pair_rows(c):
    return pl.ds(pl.multiple_of(c * PAIR, PAIR), PAIR)


def across(row):
    return jnp.transpose(jnp.broadcast_to(row, (CHUNK, CHUNK)))


def scores_of(left, right):
    return lax.dot_general(left, right, (((1,), (1,)), ((), ())), preferred_element_type=jnp.float32)


def log_of(total):
    return jnp.where(
        total < math.exp(-SHIFT),
        jnp.log1p(jnp.minimum(total, math.exp(-SHIFT)) * math.exp(SHIFT)),
        SHIFT + jnp.log(total + math.exp(-SHIFT)),
    )


def each_chunk(body):
    def step(c, carry):
        body(c)
        return carry

    lax.fori_loop(0, CHUNKS, step, 0)


def each_pair(body):
    def step(c, carry):
        body(c)
        return carry

    lax.fori_loop(0, PAIRS, step, 0)


def kernel(
    x_ref, cluster_ref, total_ref, mean_ref,
    raw, own, near, far, third, other, tags, columns, row_sums, col_sums, row_counts, masks, own_part, parts, parts_in, sums, sums_in,
    raw_sem, tags_sem, own_send, near_recv, relay_send, far_recv, relay2_send, third_recv, other_send, other_recv,
    parts_send, parts_recv, sums_send, sums_recv,
):
    gx, gy = lax.axis_index("gx"), lax.axis_index("gy")
    sizes = (lax.axis_size("gx"), lax.axis_size("gy"))
    devices = sizes[0] * sizes[1]
    me = gx * sizes[1] + gy

    d = lax.rem(me, PERIOD)
    leftward = (d >= 1) & (d <= 8)
    way = jnp.where(leftward, 1, -1)
    seat = jnp.where(leftward, d - 1, lax.rem(PERIOD - d, PERIOD))
    chain = jnp.where(leftward, RIGHT, LEFT)
    side = 1 - chain
    passes_own_back = (seat <= 2) | (seat == 7)
    has_c2 = seat <= 6
    has_c3 = seat <= 3
    has_p1 = seat <= 3
    first_seat = seat == 0
    passes_c2 = (seat >= 1) & (seat <= 4)
    lends_c2 = (seat >= 4) & (seat <= 6)
    has_other = (seat >= 1) & (seat <= 3)

    def block(offset):
        return lax.rem(me + (offset + devices), devices)

    def device(offset):
        place = block(offset)
        return (place // sizes[1], lax.rem(place, sizes[1]))

    def chunk(n):
        return jnp.where(leftward, n, CHUNKS - 1 - n)

    def pair(n):
        return jnp.where(leftward, n, PAIRS - 1 - n)

    other_core = (gx + 1 - 2 * lax.rem(gx, 2), gy)

    def raw_copy(c):
        return pltpu.make_async_copy(x_ref.at[chunk_rows(c)], raw.at[chunk_rows(c)], raw_sem.at[c])

    def tags_copy(k):
        offset = AWAY if k == X else k - REACH
        return pltpu.make_async_copy(cluster_ref.at[block(offset * way)], tags.at[k], tags_sem.at[k])

    def remote(src, dst, send_sem, recv_sem, to):
        return pltpu.make_async_remote_copy(
            src_ref=src, dst_ref=dst, send_sem=send_sem, recv_sem=recv_sem, device_id=to, device_id_type=MESH
        )

    def own_copy(which, c):
        rows = chunk_rows(c)
        return remote(
            own.at[rows], near.at[which, rows], own_send.at[which, c], near_recv.at[which, c], device(1 - 2 * which)
        )

    def relay_copy(which, c):
        rows = chunk_rows(c)
        return remote(
            near.at[which, rows], far.at[which, rows], relay_send.at[c], far_recv.at[which, c], device(1 - 2 * which)
        )

    def relay2_copy(which, c):
        rows = chunk_rows(c)
        return remote(
            far.at[which, rows], third.at[which, rows], relay2_send.at[c], third_recv.at[which, c], device(1 - 2 * which)
        )

    def other_copy(c):
        rows = chunk_rows(c)
        return remote(far.at[chain, rows], other.at[rows], other_send.at[c], other_recv.at[c], other_core)

    raw_copy(chunk(0)).start()
    barrier = pltpu.get_barrier_semaphore()
    others = [k for k in range(-REACH, REACH + 1) if k != 0]
    met = [device(k) for k in others + [-AWAY, AWAY]] + [other_core]
    for to in met:
        pl.semaphore_signal(barrier, inc=1, device_id=to, device_id_type=MESH)
    for n in range(1, CHUNKS):
        raw_copy(chunk(n)).start()
    for k in range(2 * REACH + 2):
        tags_copy(k).start()

    def normalise(c):
        raw_copy(c).wait()

        def some(g, carry):
            rows = pl.ds(pl.multiple_of(c * CHUNK + g * 16, 16), 16)
            values = raw[rows].astype(jnp.float32)
            scale = lax.rsqrt(jnp.sum(values * values, axis=1, keepdims=True) + EPSILON)
            own[rows] = (values * scale).astype(jnp.bfloat16)
            return carry

        lax.fori_loop(0, CHUNK // 16, some, 0, unroll=2)

    def send_late(n):
        for h in range(2):
            own_copy(side, chunk(CHUNKS - 1 - 2 * n - h)).start()

    normalise(chunk(0))
    pl.semaphore_wait(barrier, len(met))
    own_copy(chain, chunk(0)).start()

    def send_step(n, carry):
        normalise(chunk(n))
        own_copy(chain, chunk(n)).start()
        return carry

    lax.fori_loop(1, CHUNKS, send_step, 0)

    @pl.when(seat == 7)
    def _():
        each_pair(send_late)

    row_sums[...] = jnp.zeros_like(row_sums)
    col_sums[...] = jnp.zeros_like(col_sums)
    for k in range(2 * REACH + 2):
        tags_copy(k).wait()

    def columns_of(c):
        for kind, at in DOWN.items():
            columns[at, chunk_rows(c)] = across(tags[kind, pl.ds(c, 1), :])

    each_chunk(columns_of)

    mine = tags[S]

    def edge_tag(k):
        numbers = tags[REACH + k * way]
        at = numbers[CHUNKS - 1 : CHUNKS, CHUNK - 1 : CHUNK] if k < 0 else numbers[0:1, 0:1]
        return jnp.broadcast_to(at, (CHUNKS, CHUNK))

    def total_of(values):
        return jnp.broadcast_to(jnp.sum(values, keepdims=True), (CHUNKS, CHUNK))

    def own_totals(column_values):
        totals = []
        for j in range(CHUNKS):

            def add(c, acc):
                same = columns[DOWN[S], chunk_rows(c)] == tags[S, j : j + 1, :]
                picked = jnp.where(same, column_values(c), 0.0)
                return acc + jnp.sum(picked.reshape(CHUNK // 8, 8, CHUNK), axis=0)

            acc = lax.fori_loop(0, CHUNKS, add, jnp.zeros((8, CHUNK), jnp.float32), unroll=True)
            totals.append(jnp.sum(acc, axis=0, keepdims=True))
        return jnp.concatenate(totals, axis=0)

    counts = own_totals(lambda c: 1.0)
    for k in others:
        edge = edge_tag(k)
        many = total_of(jnp.where(tags[REACH + k * way] == edge, 1.0, 0.0))
        counts = counts + jnp.where(mine == edge, many, 0.0)
        masks[others.index(k)] = jnp.where(mine == edge, 1.0, 0.0)
    row_counts[...] = counts
    first_tag = jnp.broadcast_to(mine[0:1, 0:1], (CHUNKS, CHUNK))
    last_tag = jnp.broadcast_to(mine[CHUNKS - 1 : CHUNKS, CHUNK - 1 : CHUNK], (CHUNKS, CHUNK))
    masks[len(others)] = jnp.where(mine == first_tag, 1.0, 0.0)
    masks[len(others) + 1] = jnp.where(mine == last_tag, 1.0, 0.0)

    refs = {S: own, C1: near.at[chain], C2: far.at[chain], C3: third.at[chain], P1: near.at[side], P2: far.at[side], X: other}

    def piece(arrived, c, resident, rows, size):
        scores = scores_of(refs[resident][rows], refs[arrived][pair_rows(c)])
        numbers = columns[DOWN[resident], rows]
        total = None
        for w in range(2):
            at = pl.ds(2 * c + w, 1)
            live = numbers == tags[arrived, at, :]
            if arrived == resident:
                place = lax.broadcasted_iota(jnp.int32, (size, CHUNK), 0) - (2 * c + w) * CHUNK
                live = live & (place != lax.broadcasted_iota(jnp.int32, (size, CHUNK), 1))
            cover = jnp.where(live, jnp.exp2(scores[:, w * CHUNK : (w + 1) * CHUNK] * GAIN - DROP), 0.0)
            total = cover if total is None else total + cover
            col_sums[ACROSS[arrived], at] += jnp.sum(cover.reshape(size // 8, 8, CHUNK), axis=0)[None]
        if arrived != resident:
            row_sums[DOWN[resident], rows] += total

    def strip(arrived, c, resident):
        piece(arrived, c, resident, pl.ds(0, ROWS), ROWS)

    def pieces(first, last, arrived, c_of, resident, r_of):
        def some(j, carry):
            piece(arrived, c_of(j), resident, pair_rows(r_of(j)), PAIR)
            return carry

        lax.fori_loop(first, last, some, 0)

    def sums_of(kind):
        total = None
        if kind in ACROSS:
            total = jnp.sum(col_sums[ACROSS[kind]], axis=1)
        if kind in DOWN:
            rows = [row_sums[DOWN[kind], c * CHUNK : (c + 1) * CHUNK] for c in range(CHUNKS)]
            total = total + jnp.concatenate([jnp.sum(jnp.transpose(r), axis=0, keepdims=True) for r in rows], axis=0)
        return total

    def part_copy(kind):
        offset = AWAY if kind == X else kind - REACH
        at = PART_OFFSETS.index(offset)
        at = jnp.where(leftward, at, len(PART_OFFSETS) - 1 - at)
        return at, remote(parts.at[at], parts_in.at[at], parts_send.at[at], parts_recv.at[at], device(offset * way))

    def send_part(kind):
        at, copy = part_copy(kind)
        parts[at] = sums_of(kind)
        copy.start()

    def part_comes(offset):
        at = lax.rem(d + (PERIOD - offset), PERIOD)
        left = (at >= 1) & (at <= 8)
        there = jnp.where(left, at - 1, lax.rem(PERIOD - at, PERIOD))
        rules = {1: there >= 0, 2: there <= 6, 3: there <= 3, -1: there <= 3, -2: there == 0, AWAY: (there >= 1) & (there <= 3)}
        comes = []
        if offset in rules:
            comes.append(left & rules[offset])
        if -offset in rules:
            comes.append(jnp.logical_not(left) & rules[-offset])
        return comes[0] if len(comes) == 1 else comes[0] | comes[1]

    def chunks_sent(c):
        own_copy(chain, c).wait_send()
        @pl.when(jnp.logical_not(passes_c2))
        def _():
            relay_copy(chain, c).wait_send()

        @pl.when(passes_own_back)
        def _():
            own_copy(side, c).wait_send()

        @pl.when(passes_c2)
        def _():
            relay2_copy(chain, c).wait_send()

        @pl.when(lends_c2)
        def _():
            other_copy(c).wait_send()

    each_pair(lambda c: strip(S, c, S))

    def after_relay(n, ahead):
        @pl.when(n == 0)
        def _():
            for early in range(ahead):
                relay_copy(chain, chunk(early)).wait_send()

        @pl.when(n + ahead < CHUNKS)
        def _():
            relay_copy(chain, chunk(n + ahead)).wait_send()

    def near_step(n):
        for h in range(2):
            c = chunk(2 * n + h)
            own_copy(chain, c).wait_recv()

            @pl.when(seat != 0)
            def _():
                relay_copy(chain, c).start()

        @pl.when(d != 9)
        def _():
            strip(C1, pair(n), S)

    each_pair(near_step)

    @pl.when(seat >= 1)
    def _():
        send_part(C1)

    @pl.when(has_c2)
    def _():
        def far_step(n):
            for h in range(2):
                c = chunk(2 * n + h)
                relay_copy(chain, c).wait_recv()

                @pl.when(seat == 0)
                def _():
                    relay_copy(chain, c).start()

                @pl.when(passes_c2)
                def _():
                    after_relay(2 * n + h, 2)
                    relay2_copy(chain, c).start()

                @pl.when(lends_c2)
                def _():
                    other_copy(c).start()

            @pl.when((seat <= 2) & (n >= 2))
            def _():
                send_late(n - 2)

            strip(C2, pair(n), S)

        each_pair(far_step)

        @pl.when(seat >= 4)
        def _():
            send_part(C2)

    @pl.when(seat <= 2)
    def _():
        send_late(2)
        send_late(3)

    @pl.when(has_other)
    def _():
        def other_step(n):
            last = PAIRS - 1 - n
            for h in range(2):
                other_copy(chunk(2 * last + 1 - h)).wait_recv()
            pieces(last, PAIRS, X, lambda j: pair(last), C2, pair)

        each_pair(other_step)

    def side_step(n):
        last = PAIRS - 1 - n
        for h in range(2):
            own_copy(side, chunk(2 * last + 1 - h)).wait_recv()
        strip(P1, pair(last), C2)

    @pl.when(first_seat)
    def _():
        def first_step(n):
            side_step(n)
            strip(P1, pair(PAIRS - 1 - n), C1)

            @pl.when(d == 1)
            def _():
                strip(P1, pair(PAIRS - 1 - n), S)

        each_pair(first_step)

    @pl.when(has_c3)
    def _():
        def third_step(n):
            last = PAIRS - 1 - n
            for h in range(2):
                relay2_copy(chain, chunk(2 * n + h)).wait_recv()

            @pl.when(seat == 3)
            def _():
                strip(C3, pair(n), S)

            @pl.when(has_other & (d != 13))
            def _():
                strip(C3, pair(n), X)

            @pl.when(has_other & (n == PAIRS - 1))
            def _():
                send_part(X)

            @pl.when(has_other)
            def _():
                side_step(n)

            pieces(jnp.maximum(n, last), PAIRS, C3, lambda j: pair(n), P1, pair)
            pieces(0, jnp.minimum(n, last + 1), C3, pair, P1, lambda j: pair(last))

            @pl.when(first_seat & (n == PAIRS - 1))
            def _():
                send_part(C3)
                send_part(P1)

            @pl.when(first_seat)
            def _():
                for h in range(2):
                    relay_copy(side, chunk(2 * last + 1 - h)).wait_recv()
                pieces(n, PAIRS, P2, lambda j: pair(last), C2, lambda j: pair(PAIRS - 1 - j))

                @pl.when(d == 1)
                def _():
                    strip(P2, pair(last), C1)

        each_pair(third_step)

    for kind, sends in ((C3, has_other), (P2, first_seat), (C2, has_c2 & (seat <= 3)), (P1, has_other), (C1, first_seat)):

        @pl.when(sends)
        def _():
            send_part(kind)

    own_part[...] = sums_of(S)
    each_chunk(chunks_sent)

    for k, offset in enumerate(PART_OFFSETS):

        @pl.when(part_comes(offset))
        def _():
            remote(parts.at[k], parts_in.at[k], parts_send.at[k], parts_recv.at[k], device(offset)).wait_recv()
            own_part[...] += parts_in[k]

    total = own_part[...]
    cover = log_of(total)
    total_ref[...] = total

    for k in range(2):
        sums[k] = total_of(masks[len(others) + k] * cover)

    def sums_copy(k):
        at = others.index(k)
        return remote(sums.at[0 if k < 0 else 1, 0:1], sums_in.at[at, 0:1], sums_send.at[at], sums_recv.at[at], device(k))

    for k in sorted(others, key=abs, reverse=True):
        sums_copy(k).start()
    for kind, sends in ((C1, seat >= 0), (C2, has_c2), (C3, has_c3), (P1, has_p1), (P2, first_seat), (X, has_other)):

        @pl.when(sends)
        def _():
            part_copy(kind)[1].wait_send()

    for c in range(CHUNKS):
        row_sums[0, c * CHUNK : (c + 1) * CHUNK] = across(cover[c : c + 1])
    cluster_sums = own_totals(lambda c: row_sums[0, chunk_rows(c)])
    for k in others:
        sums_copy(k).wait_recv()
        cluster_sums = cluster_sums + masks[others.index(-k)] * sums_in[others.index(k), 0:1]
    mean_ref[...] = cluster_sums / row_counts[...]

    for k in others:
        sums_copy(k).wait_send()


def per_device(embeddings, cluster):
    rows, width = embeddings.shape
    vmem = pl.BlockSpec(memory_space=pltpu.VMEM)
    hbm = pl.BlockSpec(memory_space=pltpu.HBM)
    dma = pltpu.SemaphoreType.DMA
    small = (CHUNKS, CHUNK)
    total, mean = pl.pallas_call(
        kernel,
        out_shape=[jax.ShapeDtypeStruct(small, jnp.float32)] * 2,
        in_specs=[hbm, hbm],
        out_specs=[vmem, vmem],
        scratch_shapes=[
            pltpu.VMEM((rows, width), jnp.bfloat16),
            pltpu.VMEM((rows, width), jnp.bfloat16),
            pltpu.VMEM((2, rows, width), jnp.bfloat16),
            pltpu.VMEM((2, rows, width), jnp.bfloat16),
            pltpu.VMEM((2, rows, width), jnp.bfloat16),
            pltpu.VMEM((rows, width), jnp.bfloat16),
            pltpu.VMEM((2 * REACH + 2, *small), jnp.int32),
            pltpu.VMEM((len(DOWN), rows, CHUNK), jnp.int32),
            pltpu.VMEM((len(DOWN), rows, CHUNK), jnp.float32),
            pltpu.VMEM((len(ACROSS), CHUNKS, 8, CHUNK), jnp.float32),
            pltpu.VMEM(small, jnp.float32),
            pltpu.VMEM((2 * REACH + 2, *small), jnp.float32),
            pltpu.VMEM(small, jnp.float32),
            pltpu.VMEM((len(PART_OFFSETS), *small), jnp.float32),
            pltpu.VMEM((len(PART_OFFSETS), *small), jnp.float32),
            pltpu.VMEM((2, *small), jnp.float32),
            pltpu.VMEM((2 * REACH, *small), jnp.float32),
            dma((CHUNKS,)),
            dma((2 * REACH + 2,)),
            dma((2, CHUNKS)),
            dma((2, CHUNKS)),
            dma((CHUNKS,)),
            dma((2, CHUNKS)),
            dma((CHUNKS,)),
            dma((2, CHUNKS)),
            dma((CHUNKS,)),
            dma((CHUNKS,)),
            dma((len(PART_OFFSETS),)),
            dma((len(PART_OFFSETS),)),
            dma((2 * REACH,)),
            dma((2 * REACH,)),
        ],
        compiler_params=pltpu.CompilerParams(
            collective_id=0, has_side_effects=True, vmem_limit_bytes=53 << 20
        ),
        name="cover",
    )(embeddings, cluster.reshape(-1, *small))
    cover = log_of(total.reshape(rows))
    return cover, cover - mean.reshape(rows)


def solution(mesh):
    placed = (P(("gx", "gy"), None), P())
    return jax.shard_map(
        per_device,
        mesh=mesh,
        in_specs=placed,
        out_specs=(P(("gx", "gy")), P(("gx", "gy"))),
        check_vma=False,
    )
```

```python
import math

import jax
import jax.numpy as jnp
from jax import lax
from jax.experimental import pallas as pl
from jax.experimental.pallas import tpu as pltpu
from jax.sharding import PartitionSpec as P

MESH = pl.DeviceIdType.MESH
INVERSE_TEMP = 100.0
EPSILON = 1e-06
SHIFT = 32.0
GAIN = INVERSE_TEMP * math.log2(math.e)
DROP = SHIFT * math.log2(math.e)

ROWS = 1024
CHUNK = 128
CHUNKS = ROWS // CHUNK
LEFT, RIGHT = 0, 1
REACH = 4
PERIOD = 16

S, C1, C2, C3, P1, P2, X = REACH, REACH + 1, REACH + 2, REACH + 3, REACH - 1, REACH - 2, 2 * REACH + 1
AWAY = 6
PART_OFFSETS = [-AWAY, -3, -2, -1, 1, 2, 3, AWAY]
PAIR = 2 * CHUNK
PAIRS = ROWS // PAIR
DOWN = {S: 0, C1: 1, C2: 2, P1: 3, X: 4}
ACROSS = {S: 0, C1: 1, C2: 2, C3: 3, P1: 4, P2: 5, X: 6}


def chunk_rows(c):
    return pl.ds(pl.multiple_of(c * CHUNK, CHUNK), CHUNK)


def pair_rows(c):
    return pl.ds(pl.multiple_of(c * PAIR, PAIR), PAIR)


def across(row):
    return jnp.transpose(jnp.broadcast_to(row, (CHUNK, CHUNK)))


def scores_of(left, right):
    return lax.dot_general(left, right, (((1,), (1,)), ((), ())), preferred_element_type=jnp.float32)


def log_of(total):
    return jnp.where(
        total < math.exp(-SHIFT),
        jnp.log1p(jnp.minimum(total, math.exp(-SHIFT)) * math.exp(SHIFT)),
        SHIFT + jnp.log(total + math.exp(-SHIFT)),
    )


def each_chunk(body):
    def step(c, carry):
        body(c)
        return carry

    lax.fori_loop(0, CHUNKS, step, 0)


def each_pair(body):
    def step(c, carry):
        body(c)
        return carry

    lax.fori_loop(0, PAIRS, step, 0)


def kernel(
    x_ref, cluster_ref, total_ref, mean_ref,
    raw, own, near, far, third, other, tags, columns, row_sums, col_sums, row_counts, masks, own_part, parts, parts_in, sums, sums_in,
    raw_sem, tags_sem, own_send, near_recv, relay_send, far_recv, relay2_send, third_recv, other_send, other_recv,
    parts_send, parts_recv, sums_send, sums_recv,
):
    gx, gy = lax.axis_index("gx"), lax.axis_index("gy")
    sizes = (lax.axis_size("gx"), lax.axis_size("gy"))
    devices = sizes[0] * sizes[1]
    me = gx * sizes[1] + gy

    d = lax.rem(me, PERIOD)
    leftward = (d >= 1) & (d <= 8)
    way = jnp.where(leftward, 1, -1)
    seat = jnp.where(leftward, d - 1, lax.rem(PERIOD - d, PERIOD))
    chain = jnp.where(leftward, RIGHT, LEFT)
    side = 1 - chain
    passes_own_back = (seat <= 2) | (seat == 7)
    has_c2 = seat <= 6
    has_c3 = seat <= 3
    has_p1 = seat <= 3
    first_seat = seat == 0
    passes_c2 = (seat >= 1) & (seat <= 4)
    lends_c2 = (seat >= 4) & (seat <= 6)
    has_other = (seat >= 1) & (seat <= 3)

    def block(offset):
        return lax.rem(me + (offset + devices), devices)

    def device(offset):
        place = block(offset)
        return (place // sizes[1], lax.rem(place, sizes[1]))

    def chunk(n):
        return jnp.where(leftward, n, CHUNKS - 1 - n)

    def pair(n):
        return jnp.where(leftward, n, PAIRS - 1 - n)

    other_core = (gx + 1 - 2 * lax.rem(gx, 2), gy)

    def raw_copy(c):
        return pltpu.make_async_copy(x_ref.at[chunk_rows(c)], raw.at[chunk_rows(c)], raw_sem.at[c])

    def tags_copy(k):
        offset = AWAY if k == X else k - REACH
        return pltpu.make_async_copy(cluster_ref.at[block(offset * way)], tags.at[k], tags_sem.at[k])

    def remote(src, dst, send_sem, recv_sem, to):
        return pltpu.make_async_remote_copy(
            src_ref=src, dst_ref=dst, send_sem=send_sem, recv_sem=recv_sem, device_id=to, device_id_type=MESH
        )

    def own_copy(which, c):
        rows = chunk_rows(c)
        return remote(
            own.at[rows], near.at[which, rows], own_send.at[which, c], near_recv.at[which, c], device(1 - 2 * which)
        )

    def relay_copy(which, c):
        rows = chunk_rows(c)
        return remote(
            near.at[which, rows], far.at[which, rows], relay_send.at[c], far_recv.at[which, c], device(1 - 2 * which)
        )

    def relay2_copy(which, c):
        rows = chunk_rows(c)
        return remote(
            far.at[which, rows], third.at[which, rows], relay2_send.at[c], third_recv.at[which, c], device(1 - 2 * which)
        )

    def other_copy(c):
        rows = chunk_rows(c)
        return remote(far.at[chain, rows], other.at[rows], other_send.at[c], other_recv.at[c], other_core)

    raw_copy(chunk(0)).start()
    barrier = pltpu.get_barrier_semaphore()
    others = [k for k in range(-REACH, REACH + 1) if k != 0]
    met = [device(k) for k in others + [-AWAY, AWAY]] + [other_core]
    for to in met:
        pl.semaphore_signal(barrier, inc=1, device_id=to, device_id_type=MESH)
    for n in range(1, CHUNKS):
        raw_copy(chunk(n)).start()
    for k in range(2 * REACH + 2):
        tags_copy(k).start()

    def normalise(c):
        raw_copy(c).wait()

        def some(g, carry):
            rows = pl.ds(pl.multiple_of(c * CHUNK + g * 16, 16), 16)
            values = raw[rows].astype(jnp.float32)
            scale = lax.rsqrt(jnp.sum(values * values, axis=1, keepdims=True) + EPSILON)
            own[rows] = (values * scale).astype(jnp.bfloat16)
            return carry

        lax.fori_loop(0, CHUNK // 16, some, 0, unroll=True)

    def send_late(n):
        for h in range(2):
            own_copy(side, chunk(CHUNKS - 1 - 2 * n - h)).start()

    normalise(chunk(0))
    pl.semaphore_wait(barrier, len(met))
    own_copy(chain, chunk(0)).start()

    def send_step(n, carry):
        normalise(chunk(n))
        own_copy(chain, chunk(n)).start()
        return carry

    lax.fori_loop(1, CHUNKS, send_step, 0)

    @pl.when(seat == 7)
    def _():
        each_pair(send_late)

    row_sums[...] = jnp.zeros_like(row_sums)
    col_sums[...] = jnp.zeros_like(col_sums)
    for k in range(2 * REACH + 2):
        tags_copy(k).wait()

    def columns_of(c):
        for kind, at in DOWN.items():
            columns[at, chunk_rows(c)] = across(tags[kind, pl.ds(c, 1), :])

    each_chunk(columns_of)

    mine = tags[S]

    def edge_tag(k):
        numbers = tags[REACH + k * way]
        at = numbers[CHUNKS - 1 : CHUNKS, CHUNK - 1 : CHUNK] if k < 0 else numbers[0:1, 0:1]
        return jnp.broadcast_to(at, (CHUNKS, CHUNK))

    def total_of(values):
        return jnp.broadcast_to(jnp.sum(values, keepdims=True), (CHUNKS, CHUNK))

    def own_totals(column_values):
        totals = []
        for j in range(CHUNKS):

            def add(c, acc):
                same = columns[DOWN[S], chunk_rows(c)] == tags[S, j : j + 1, :]
                picked = jnp.where(same, column_values(c), 0.0)
                return acc + jnp.sum(picked.reshape(CHUNK // 8, 8, CHUNK), axis=0)

            acc = lax.fori_loop(0, CHUNKS, add, jnp.zeros((8, CHUNK), jnp.float32), unroll=True)
            totals.append(jnp.sum(acc, axis=0, keepdims=True))
        return jnp.concatenate(totals, axis=0)

    counts = own_totals(lambda c: 1.0)
    for k in others:
        edge = edge_tag(k)
        many = total_of(jnp.where(tags[REACH + k * way] == edge, 1.0, 0.0))
        counts = counts + jnp.where(mine == edge, many, 0.0)
        masks[others.index(k)] = jnp.where(mine == edge, 1.0, 0.0)
    row_counts[...] = counts
    first_tag = jnp.broadcast_to(mine[0:1, 0:1], (CHUNKS, CHUNK))
    last_tag = jnp.broadcast_to(mine[CHUNKS - 1 : CHUNKS, CHUNK - 1 : CHUNK], (CHUNKS, CHUNK))
    masks[len(others)] = jnp.where(mine == first_tag, 1.0, 0.0)
    masks[len(others) + 1] = jnp.where(mine == last_tag, 1.0, 0.0)

    refs = {S: own, C1: near.at[chain], C2: far.at[chain], C3: third.at[chain], P1: near.at[side], P2: far.at[side], X: other}

    def piece(arrived, c, resident, rows, size):
        scores = scores_of(refs[resident][rows], refs[arrived][pair_rows(c)])
        numbers = columns[DOWN[resident], rows]
        total = None
        for w in range(2):
            at = pl.ds(2 * c + w, 1)
            live = numbers == tags[arrived, at, :]
            if arrived == resident:
                place = lax.broadcasted_iota(jnp.int32, (size, CHUNK), 0) - (2 * c + w) * CHUNK
                live = live & (place != lax.broadcasted_iota(jnp.int32, (size, CHUNK), 1))
            cover = jnp.where(live, jnp.exp2(scores[:, w * CHUNK : (w + 1) * CHUNK] * GAIN - DROP), 0.0)
            total = cover if total is None else total + cover
            col_sums[ACROSS[arrived], at] += jnp.sum(cover.reshape(size // 8, 8, CHUNK), axis=0)[None]
        if arrived != resident:
            row_sums[DOWN[resident], rows] += total

    def strip(arrived, c, resident):
        piece(arrived, c, resident, pl.ds(0, ROWS), ROWS)

    def pieces(first, last, arrived, c_of, resident, r_of):
        def some(j, carry):
            piece(arrived, c_of(j), resident, pair_rows(r_of(j)), PAIR)
            return carry

        lax.fori_loop(first, last, some, 0)

    def sums_of(kind):
        total = None
        if kind in ACROSS:
            total = jnp.sum(col_sums[ACROSS[kind]], axis=1)
        if kind in DOWN:
            rows = [row_sums[DOWN[kind], c * CHUNK : (c + 1) * CHUNK] for c in range(CHUNKS)]
            total = total + jnp.concatenate([jnp.sum(jnp.transpose(r), axis=0, keepdims=True) for r in rows], axis=0)
        return total

    def part_copy(kind):
        offset = AWAY if kind == X else kind - REACH
        at = PART_OFFSETS.index(offset)
        at = jnp.where(leftward, at, len(PART_OFFSETS) - 1 - at)
        return at, remote(parts.at[at], parts_in.at[at], parts_send.at[at], parts_recv.at[at], device(offset * way))

    def send_part(kind):
        at, copy = part_copy(kind)
        parts[at] = sums_of(kind)
        copy.start()

    def part_comes(offset):
        at = lax.rem(d + (PERIOD - offset), PERIOD)
        left = (at >= 1) & (at <= 8)
        there = jnp.where(left, at - 1, lax.rem(PERIOD - at, PERIOD))
        rules = {1: there >= 0, 2: there <= 6, 3: there <= 3, -1: there <= 3, -2: there == 0, AWAY: (there >= 1) & (there <= 3)}
        comes = []
        if offset in rules:
            comes.append(left & rules[offset])
        if -offset in rules:
            comes.append(jnp.logical_not(left) & rules[-offset])
        return comes[0] if len(comes) == 1 else comes[0] | comes[1]

    def chunks_sent(c):
        own_copy(chain, c).wait_send()
        relay_copy(chain, c).wait_send()

        @pl.when(passes_own_back)
        def _():
            own_copy(side, c).wait_send()

        @pl.when(passes_c2)
        def _():
            relay2_copy(chain, c).wait_send()

        @pl.when(lends_c2)
        def _():
            other_copy(c).wait_send()

    each_pair(lambda c: strip(S, c, S))

    def near_step(n):
        for h in range(2):
            c = chunk(2 * n + h)
            own_copy(chain, c).wait_recv()

            @pl.when(seat != 0)
            def _():
                relay_copy(chain, c).start()

        @pl.when(d != 9)
        def _():
            strip(C1, pair(n), S)

    each_pair(near_step)

    @pl.when(seat >= 1)
    def _():
        send_part(C1)

    @pl.when(has_c2)
    def _():
        def far_step(n):
            for h in range(2):
                c = chunk(2 * n + h)
                relay_copy(chain, c).wait_recv()

                @pl.when(seat == 0)
                def _():
                    relay_copy(chain, c).start()

                @pl.when(passes_c2)
                def _():
                    relay2_copy(chain, c).start()

                @pl.when(lends_c2)
                def _():
                    other_copy(c).start()

            @pl.when((seat <= 2) & (n >= 2))
            def _():
                send_late(n - 2)

            strip(C2, pair(n), S)

        each_pair(far_step)

        @pl.when(seat >= 4)
        def _():
            send_part(C2)

    @pl.when(seat <= 2)
    def _():
        send_late(2)
        send_late(3)

    @pl.when(has_other)
    def _():
        def other_step(n):
            last = PAIRS - 1 - n
            for h in range(2):
                other_copy(chunk(2 * last + 1 - h)).wait_recv()
            pieces(last, PAIRS, X, lambda j: pair(last), C2, pair)

        each_pair(other_step)

    def side_step(n):
        last = PAIRS - 1 - n
        for h in range(2):
            own_copy(side, chunk(2 * last + 1 - h)).wait_recv()
        strip(P1, pair(last), C2)

    @pl.when(first_seat)
    def _():
        def first_step(n):
            side_step(n)
            strip(P1, pair(PAIRS - 1 - n), C1)

            @pl.when(d == 1)
            def _():
                strip(P1, pair(PAIRS - 1 - n), S)

        each_pair(first_step)

    @pl.when(has_c3)
    def _():
        def third_step(n):
            last = PAIRS - 1 - n
            for h in range(2):
                relay2_copy(chain, chunk(2 * n + h)).wait_recv()

            @pl.when(seat == 3)
            def _():
                strip(C3, pair(n), S)

            @pl.when(has_other & (d != 13))
            def _():
                strip(C3, pair(n), X)

            @pl.when(has_other & (n == PAIRS - 1))
            def _():
                send_part(X)

            @pl.when(has_other)
            def _():
                side_step(n)

            pieces(jnp.maximum(n, last), PAIRS, C3, lambda j: pair(n), P1, pair)
            pieces(0, jnp.minimum(n, last + 1), C3, pair, P1, lambda j: pair(last))

            @pl.when(first_seat & (n == PAIRS - 1))
            def _():
                send_part(C3)
                send_part(P1)

            @pl.when(first_seat)
            def _():
                for h in range(2):
                    relay_copy(side, chunk(2 * last + 1 - h)).wait_recv()
                pieces(n, PAIRS, P2, lambda j: pair(last), C2, lambda j: pair(PAIRS - 1 - j))

                @pl.when(d == 1)
                def _():
                    strip(P2, pair(last), C1)

        each_pair(third_step)

    for kind, sends in ((C3, has_other), (P2, first_seat), (C2, has_c2 & (seat <= 3)), (P1, has_other), (C1, first_seat)):

        @pl.when(sends)
        def _():
            send_part(kind)

    own_part[...] = sums_of(S)
    each_chunk(chunks_sent)

    for k, offset in enumerate(PART_OFFSETS):

        @pl.when(part_comes(offset))
        def _():
            remote(parts.at[k], parts_in.at[k], parts_send.at[k], parts_recv.at[k], device(offset)).wait_recv()
            own_part[...] += parts_in[k]

    total = own_part[...]
    cover = log_of(total)
    total_ref[...] = total

    for k in range(2):
        sums[k] = total_of(masks[len(others) + k] * cover)

    def sums_copy(k):
        at = others.index(k)
        return remote(sums.at[0 if k < 0 else 1, 0:1], sums_in.at[at, 0:1], sums_send.at[at], sums_recv.at[at], device(k))

    for k in sorted(others, key=abs, reverse=True):
        sums_copy(k).start()
    for kind, sends in ((C1, seat >= 0), (C2, has_c2), (C3, has_c3), (P1, has_p1), (P2, first_seat), (X, has_other)):

        @pl.when(sends)
        def _():
            part_copy(kind)[1].wait_send()

    for c in range(CHUNKS):
        row_sums[0, c * CHUNK : (c + 1) * CHUNK] = across(cover[c : c + 1])
    cluster_sums = own_totals(lambda c: row_sums[0, chunk_rows(c)])
    for k in others:
        sums_copy(k).wait_recv()
        cluster_sums = cluster_sums + masks[others.index(-k)] * sums_in[others.index(k), 0:1]
    mean_ref[...] = cluster_sums / row_counts[...]

    for k in others:
        sums_copy(k).wait_send()


def per_device(embeddings, cluster):
    rows, width = embeddings.shape
    vmem = pl.BlockSpec(memory_space=pltpu.VMEM)
    hbm = pl.BlockSpec(memory_space=pltpu.HBM)
    dma = pltpu.SemaphoreType.DMA
    small = (CHUNKS, CHUNK)
    total, mean = pl.pallas_call(
        kernel,
        out_shape=[jax.ShapeDtypeStruct(small, jnp.float32)] * 2,
        in_specs=[hbm, hbm],
        out_specs=[vmem, vmem],
        scratch_shapes=[
            pltpu.VMEM((rows, width), jnp.bfloat16),
            pltpu.VMEM((rows, width), jnp.bfloat16),
            pltpu.VMEM((2, rows, width), jnp.bfloat16),
            pltpu.VMEM((2, rows, width), jnp.bfloat16),
            pltpu.VMEM((2, rows, width), jnp.bfloat16),
            pltpu.VMEM((rows, width), jnp.bfloat16),
            pltpu.VMEM((2 * REACH + 2, *small), jnp.int32),
            pltpu.VMEM((len(DOWN), rows, CHUNK), jnp.int32),
            pltpu.VMEM((len(DOWN), rows, CHUNK), jnp.float32),
            pltpu.VMEM((len(ACROSS), CHUNKS, 8, CHUNK), jnp.float32),
            pltpu.VMEM(small, jnp.float32),
            pltpu.VMEM((2 * REACH + 2, *small), jnp.float32),
            pltpu.VMEM(small, jnp.float32),
            pltpu.VMEM((len(PART_OFFSETS), *small), jnp.float32),
            pltpu.VMEM((len(PART_OFFSETS), *small), jnp.float32),
            pltpu.VMEM((2, *small), jnp.float32),
            pltpu.VMEM((2 * REACH, *small), jnp.float32),
            dma((CHUNKS,)),
            dma((2 * REACH + 2,)),
            dma((2, CHUNKS)),
            dma((2, CHUNKS)),
            dma((CHUNKS,)),
            dma((2, CHUNKS)),
            dma((CHUNKS,)),
            dma((2, CHUNKS)),
            dma((CHUNKS,)),
            dma((CHUNKS,)),
            dma((len(PART_OFFSETS),)),
            dma((len(PART_OFFSETS),)),
            dma((2 * REACH,)),
            dma((2 * REACH,)),
        ],
        compiler_params=pltpu.CompilerParams(
            collective_id=0, has_side_effects=True, vmem_limit_bytes=53 << 20
        ),
        name="cover",
    )(embeddings, cluster.reshape(-1, *small))
    cover = log_of(total.reshape(rows))
    return cover, cover - mean.reshape(rows)


def solution(mesh):
    placed = (P(("gx", "gy"), None), P())
    return jax.shard_map(
        per_device,
        mesh=mesh,
        in_specs=placed,
        out_specs=(P(("gx", "gy")), P(("gx", "gy"))),
        check_vma=False,
    )
```
